128 devices in a mesh: section: 2 (over core), seq: 16 (over y, x), fsdp: 4 (over z).
Axes of the slice: x: 4, y: 4, z: 4, core: 2. Of those that a mesh axis runs over, the one named last changes fastest.
Arguments:
- hidden_in: bfloat16 [3, 4, 2048, 640], P(None, 'fsdp', 'seq'), may hold values from -6 to 6
- positions: int32 [3, 4, 2048], P(None, 'fsdp', 'seq'), may hold values from 0 to 4093, as said below
- segments: int32 [3, 4, 2048], P(None, 'fsdp'), may hold values from 0 to 4, as said below
- cotangent: bfloat16 [3, 4, 2048, 640], P(None, 'fsdp', 'seq'), may hold values from -6 to 6
- query_weight: bfloat16 [2, 640, 1024], P('section', 'fsdp'), may hold values from -0.25 to 0.25
- key_weight: bfloat16 [2, 640, 256], P('section', 'fsdp'), may hold values from -0.25 to 0.25
- value_weight: bfloat16 [2, 640, 256], P('section', 'fsdp'), may hold values from -0.25 to 0.25
- output_weight: bfloat16 [2, 1024, 640], P('section', 'fsdp'), may hold values from -0.1875 to 0.1875
- gate_weight: bfloat16 [2, 640, 2048], P('section', 'fsdp'), may hold values from -0.25 to 0.25
- up_weight: bfloat16 [2, 640, 2048], P('section', 'fsdp'), may hold values from -0.25 to 0.25
- down_weight: bfloat16 [2, 2048, 640], P('section', 'fsdp'), may hold values from -0.125 to 0.125
- pre_gain: bfloat16 [2, 640], P('section', 'fsdp'), may hold values from 0.5 to 1.5
- query_gain: bfloat16 [2, 256], P('section', 'fsdp'), may hold values from 0.5 to 1.5
- key_gain: bfloat16 [2, 256], P('section', 'fsdp'), may hold values from 0.5 to 1.5
- mix_gain: bfloat16 [2, 640], P('section', 'fsdp'), may hold values from 0.5 to 1.5
- ffn_gain: bfloat16 [2, 640], P('section', 'fsdp'), may hold values from 0.5 to 1.5
- out_gain: bfloat16 [2, 640], P('section', 'fsdp'), may hold values from 0.5 to 1.5
Outputs:
- section_outputs: bfloat16 [2, 3, 4, 2048, 640], P('section', None, 'fsdp', 'seq')
- input_grads: float32 [2, 3, 4, 2048, 640], P('section', None, 'fsdp', 'seq')
- query_grad: float32 [2, 640, 1024], P('section', 'fsdp')
- key_grad: float32 [2, 640, 256], P('section', 'fsdp')
- value_grad: float32 [2, 640, 256], P('section', 'fsdp')
- output_grad: float32 [2, 1024, 640], P('section', 'fsdp')
- gate_grad: float32 [2, 640, 2048], P('section', 'fsdp')
- up_grad: float32 [2, 640, 2048], P('section', 'fsdp')
- down_grad: float32 [2, 2048, 640], P('section', 'fsdp')
- pre_gain_grad: float32 [2, 640], P('section', 'fsdp')
- query_gain_grad: float32 [2, 256], P('section', 'fsdp')
- key_gain_grad: float32 [2, 256], P('section', 'fsdp')
- mix_gain_grad: float32 [2, 640], P('section', 'fsdp')
- ffn_gain_grad: float32 [2, 640], P('section', 'fsdp')
- out_gain_grad: float32 [2, 640], P('section', 'fsdp')
The draws below stay inside these ranges and needn't reach their ends.
Inputs may be any that keep to these rules, and one draw needn't show every extreme that they name: `segments`: segment numbers never fall along a sequence; in every sequence one segment begins within its first 128 tokens and ends within its last 128. `positions`: within a segment the position rises by one from token to token.
All inputs are finite; a program needn't handle non-finite values.
Results may differ from the reference program's by a relative error of at most 0.029.
Values may be sent and summed in bfloat16 or wider, within the bound.
No kernel may reach another device: no remote copies, remote signals or barrier semaphores. Data moves between devices by JAX's collectives and lax.ppermute only.
A program may use at most 256 MiB of HBM per device.

```python
import jax
import jax.numpy as jnp
from jax import lax

D = 640
FF = 2048
QH = 4
HD = 256
WINDOW = 512
MICRO = 3
SEQ_LEN = 2048
SHARD = 128
N_SECTION = 2
N_FSDP = 4


def doc_layout(key):
    rows = MICRO * N_FSDP
    keys = jax.random.split(key, 5)
    opening = jax.random.randint(keys[0], (rows, 1), 1, SHARD)
    leading = jax.random.randint(keys[1], (rows, 1), 1, opening + 1)
    closing = jax.random.randint(keys[2], (rows, 1), SEQ_LEN - SHARD + 1, SEQ_LEN)
    trailing = jax.random.randint(keys[3], (rows, 1), closing, SEQ_LEN)
    place = jnp.arange(SEQ_LEN, dtype=jnp.int32)[None, :]
    segment = (place >= leading).astype(jnp.int32) + (place >= opening).astype(jnp.int32) + (place >= closing).astype(jnp.int32) + (place >= trailing).astype(jnp.int32)
    starts = jnp.concatenate([jnp.zeros((rows, 1), jnp.int32), leading, opening, closing, trailing], axis=1)
    offsets = jax.random.randint(keys[4], (rows, 5), 0, 2048) * (jnp.arange(5) > 0).astype(jnp.int32)
    begin = jnp.take_along_axis(starts, segment, axis=1)
    carried = jnp.take_along_axis(offsets, segment, axis=1)
    position = place - begin + carried
    return (segment.reshape(MICRO, N_FSDP, SEQ_LEN), position.reshape(MICRO, N_FSDP, SEQ_LEN))


def draw_segments(key, part):
    return doc_layout(key)[0]


def draw_positions(key, part):
    return doc_layout(key)[1]


def levels(stream_key, extent, cuts, smallest, largest):
    factor_of = 1.0
    for dim, blocks in cuts:
        heights = jax.random.uniform(jax.random.fold_in(jax.random.fold_in(stream_key, 6), dim), (blocks,), jnp.float32, smallest / len(cuts), largest / len(cuts))
        factor_of = factor_of * jnp.repeat(jnp.exp(heights), extent[dim] // blocks).reshape((-1,) + (1,) * (len(extent) - 1 - dim))
    return factor_of


def bell_draw(key, extent, spread, limit, pieces=(), held_as=jnp.bfloat16):
    factor_of = levels(key, extent, pieces, -0.22, 0.18) if pieces else 1.0
    array = jax.random.normal(key, extent, jnp.float32) * spread * factor_of
    return jnp.minimum(jnp.maximum(array, -limit), limit).astype(held_as)


def setup_inputs(seed: int = 0) -> dict:
    key_of = jax.random.split(jax.random.key(seed), 18)
    return {
        "hidden_in": bell_draw(key_of[0], (MICRO, N_FSDP, SEQ_LEN, D), 1.0, 6.0, ((1, 4), (2, 16))),
        "positions": draw_positions(jax.random.fold_in(key_of[17], 71), 0),
        "segments": draw_segments(jax.random.fold_in(key_of[17], 71), 0),
        "cotangent": bell_draw(key_of[3], (MICRO, N_FSDP, SEQ_LEN, D), 1.0, 6.0, ((1, 4), (2, 16))),
        "query_weight": bell_draw(key_of[4], (N_SECTION, D, QH * HD), D ** -0.5, 0.25, ((0, 2), (1, 4))),
        "key_weight": bell_draw(key_of[5], (N_SECTION, D, HD), D ** -0.5, 0.25, ((0, 2), (1, 4))),
        "value_weight": bell_draw(key_of[6], (N_SECTION, D, HD), D ** -0.5, 0.25, ((0, 2), (1, 4))),
        "output_weight": bell_draw(key_of[7], (N_SECTION, QH * HD, D), (QH * HD) ** -0.5, 0.1875, ((0, 2), (1, 4))),
        "gate_weight": bell_draw(key_of[8], (N_SECTION, D, FF), D ** -0.5, 0.25, ((0, 2), (1, 4))),
        "up_weight": bell_draw(key_of[9], (N_SECTION, D, FF), D ** -0.5, 0.25, ((0, 2), (1, 4))),
        "down_weight": bell_draw(key_of[10], (N_SECTION, FF, D), FF ** -0.5, 0.125, ((0, 2), (1, 4))),
        "pre_gain": jnp.clip(1.0 + 0.1 * jax.random.normal(key_of[11], (N_SECTION, D), jnp.float32), 0.5, 1.5).astype(jnp.bfloat16),
        "query_gain": jnp.clip(1.0 + 0.1 * jax.random.normal(key_of[12], (N_SECTION, HD), jnp.float32), 0.5, 1.5).astype(jnp.bfloat16),
        "key_gain": jnp.clip(1.0 + 0.1 * jax.random.normal(key_of[13], (N_SECTION, HD), jnp.float32), 0.5, 1.5).astype(jnp.bfloat16),
        "mix_gain": jnp.clip(1.0 + 0.1 * jax.random.normal(key_of[14], (N_SECTION, D), jnp.float32), 0.5, 1.5).astype(jnp.bfloat16),
        "ffn_gain": jnp.clip(1.0 + 0.1 * jax.random.normal(key_of[15], (N_SECTION, D), jnp.float32), 0.5, 1.5).astype(jnp.bfloat16),
        "out_gain": jnp.clip(1.0 + 0.1 * jax.random.normal(key_of[16], (N_SECTION, D), jnp.float32), 0.5, 1.5).astype(jnp.bfloat16),
    }


EPSILON = 1e-06
ROPE_BASE = 10000.0

@jax.custom_vjp
def low(v):
    return lax.optimization_barrier(v.astype(jnp.bfloat16)).astype(jnp.float32)

@jax.custom_vjp
def low_back(v):
    return v

def low_keep(v):
    return (low(v), None)

def low_pass(kept, grad):
    return (grad,)

def back_keep(v):
    return (v, None)

def back_low(kept, grad):
    return (low(grad),)
low.defvjp(low_keep, low_pass)
low_back.defvjp(back_keep, back_low)

def precise(left, right):
    return jnp.dot(left, right, precision=lax.Precision.HIGHEST, preferred_element_type=jnp.float32)

def normalize(values, gain):
    return values * lax.rsqrt(lax.optimization_barrier(jnp.mean(values * values, axis=-1, keepdims=True)) + EPSILON) * gain

def rotate(values, places):
    half = values.shape[-1] // 2
    exponent = jnp.arange(half).astype(jnp.float32) * (2.0 / values.shape[-1])
    freqs = ROPE_BASE ** (-exponent)
    angle = places.astype(jnp.float32)[:, None] * freqs[None, :]
    cosine = jnp.cos(angle)
    sine = jnp.sin(angle)
    if values.ndim == 3:
        cosine = cosine[:, None, :]
        sine = sine[:, None, :]
    former = values[..., :half]
    latter = values[..., half:]
    return jnp.concatenate([former * cosine - latter * sine, latter * cosine + former * sine], axis=-1)

def attend(query, key, value, segment):
    length = query.shape[0]
    block = min(512, length)
    scale = HD ** (-0.5)
    pad_keys = jnp.concatenate([jnp.zeros((WINDOW, HD), jnp.float32), key], axis=0)
    pad_values = jnp.concatenate([jnp.zeros((WINDOW, HD), jnp.float32), value], axis=0)
    pad_segment = jnp.concatenate([jnp.full((WINDOW,), -1, jnp.int32), segment.astype(jnp.int32)])

    def one_block(start):
        q_rows = lax.dynamic_slice_in_dim(query, start, block, 0)
        k_rows = lax.dynamic_slice_in_dim(pad_keys, start, block + WINDOW, 0)
        v_rows = lax.dynamic_slice_in_dim(pad_values, start, block + WINDOW, 0)
        q_seg = lax.dynamic_slice_in_dim(segment.astype(jnp.int32), start, block, 0)
        k_seg = lax.dynamic_slice_in_dim(pad_segment, start, block + WINDOW, 0)
        q_place = start + jnp.arange(block).astype(jnp.int32)
        k_place = start - WINDOW + jnp.arange(block + WINDOW).astype(jnp.int32)
        gap = q_place[:, None] - k_place[None, :]
        allowed = (gap >= 0) & (gap < WINDOW) & (q_seg[:, None] == k_seg[None, :])
        raw = jnp.einsum('qhd,kd->hqk', q_rows, k_rows, precision=lax.Precision.HIGHEST)
        score = jnp.where(allowed[None], low_back(raw * scale), -1e+30)
        highest = lax.optimization_barrier(jnp.max(score, axis=-1, keepdims=True))
        expo = jnp.exp(score - highest)
        prob = expo / lax.optimization_barrier(jnp.sum(expo, axis=-1, keepdims=True))
        return jnp.einsum('hqk,kd->qhd', low(prob), v_rows, precision=lax.Precision.HIGHEST)
    starts = (jnp.arange(length // block) * block).astype(jnp.int32)
    blocks = lax.map(jax.checkpoint(one_block), starts)
    return blocks.reshape(length, QH * HD)

def layer(inputs, params, places, segment):
    query_w, key_w, value_w, output_w, gate_w, up_w, down_w, pre_g, query_g, key_g, mix_g, ffn_g, out_g = params
    length = inputs.shape[0]
    normed = low(normalize(inputs, pre_g))
    query = low_back(precise(normed, query_w)).reshape(length, QH, HD)
    key = low_back(precise(normed, key_w))
    value = low(low_back(precise(normed, value_w)))
    query = low(rotate(normalize(query, query_g), places))
    key = low(rotate(normalize(key, key_g), places))
    mixed = low(low_back(attend(query, key, value, segment)))
    branch = low_back(precise(mixed, output_w))
    middle = inputs + normalize(branch, mix_g)
    inner = low(normalize(middle, ffn_g))
    gate_act = low_back(precise(inner, gate_w))
    up_act = low_back(precise(inner, up_w))
    hidden = low(jax.nn.gelu(gate_act) * up_act)
    down = low_back(precise(hidden, down_w))
    return middle + normalize(down, out_g)

def reference(hidden_in, positions, segments, cotangent, query_weight, key_weight, value_weight, output_weight, gate_weight, up_weight, down_weight, pre_gain, query_gain, key_gain, mix_gain, ffn_gain, out_gain):
    weights = tuple((item.astype(jnp.float32) for item in (query_weight, key_weight, value_weight, output_weight, gate_weight, up_weight, down_weight, pre_gain, query_gain, key_gain, mix_gain, ffn_gain, out_gain)))
    start = hidden_in.astype(jnp.float32).reshape(-1, SEQ_LEN, D)
    places = positions.reshape(-1, SEQ_LEN)
    segment_rows = segments.reshape(-1, SEQ_LEN)

    def run(params, inputs):
        return lax.map(lambda entry: layer(entry[0], params, entry[1], entry[2]), (inputs, places, segment_rows))

    def forward(params, first, delta):
        section_zero = tuple((item[0] for item in params))
        section_one = tuple((item[1] for item in params))
        middle = low(run(section_zero, first))
        last = low(run(section_one, low_back(middle) + delta))
        return (middle, last)
    (middle, last), pull = jax.vjp(forward, weights, start, jnp.zeros_like(start))
    grads, grad_start, grad_delta = pull((jnp.zeros_like(middle), cotangent.astype(jnp.float32).reshape(-1, SEQ_LEN, D)))
    shape = (N_SECTION, MICRO, N_FSDP, SEQ_LEN, D)
    section_outputs = jnp.stack([middle, last]).reshape(shape).astype(jnp.bfloat16)
    input_grads = jnp.stack([grad_start, grad_delta]).reshape(shape)
    return (section_outputs, input_grads, grads[0], grads[1], grads[2], grads[3], grads[4], grads[5], grads[6], grads[7], grads[8], grads[9], grads[10], grads[11], grads[12])
```

```python
import jax
import jax.numpy as jnp
import numpy as np
from jax import lax
from jax.experimental import pallas as pl
from jax.experimental.pallas import tpu as pltpu
from jax.sharding import Mesh, PartitionSpec as P

WINDOW = 512
EPSILON = 1e-06
ROPE_BASE = 10000.0

RING = 4
D = 640
FF = 2048
QH = 4
HD = 256
MICRO = 3
SHARD = 128
TOKENS = MICRO * SHARD
HOPS = WINDOW // SHARD
KEYS = SHARD + WINDOW

ROWS = 256
FFN_COLS = 4096
ATTN_COLS = 1920

FFN_PLAN = ((0, 0, 160, 0, 2048, 0, 0), (1, 0, 160, 0, 2048, 0, 2048)) + tuple(
    (2, 96 * i, min(96, 512 - 96 * i), 0, 640, 160, 640 * i) for i in range(6)
)
ATTN_PLAN = (
    (0, 0, 160, 0, 1024, 0, 0),
    (1, 0, 160, 0, 256, 0, 1024),
    (2, 0, 160, 0, 256, 0, 1280),
) + tuple((3, 96 * i, min(96, 256 - 96 * i), 0, 640, 160, 640 * i) for i in range(3))

FFN_GRAD_PLAN = ((0, 0, 160, 0, 4096, 0, 0),) + tuple(
    (1, 96 * i, min(96, 512 - 96 * i), 0, 640, 160, 640 * i) for i in range(6)
)
ATTN_GRAD_PLAN = ((0, 0, 160, 0, 1536, 0, 0),) + tuple(
    (1, 96 * i, min(96, 256 - 96 * i), 0, 640, 160, 640 * i) for i in range(3)
)


def in_any(count):
    return [pl.BlockSpec(memory_space=pl.ANY)] * count


def run_copies(copies):
    for item in copies:
        item.start()
    for item in copies:
        item.wait()


def pack_shard(arrays, plan, cols):
    def body(*refs):
        sources, out, sems = refs[: len(arrays)], refs[len(arrays)], refs[len(arrays) + 1]
        run_copies(
            [
                pltpu.make_async_copy(
                    sources[a].at[pl.ds(r, n), pl.ds(c, w)],
                    out.at[pl.ds(pr, n), pl.ds(pc, w)],
                    sems.at[i],
                )
                for i, (a, r, n, c, w, pr, pc) in enumerate(plan)
            ]
        )

    return pl.pallas_call(
        body,
        in_specs=in_any(len(arrays)),
        out_specs=pl.BlockSpec(memory_space=pl.ANY),
        out_shape=jax.ShapeDtypeStruct((ROWS, cols), jnp.bfloat16),
        scratch_shapes=[pltpu.SemaphoreType.DMA((len(plan),))],
        name="pack_shard",
    )(*arrays)


def unpack_full(place, pieces, plan, shapes):
    arrays = [item[0] for item in pieces]
    jobs = []
    for index, (_, rel, first, count) in enumerate(pieces):
        for a, r, n, c, w, pr, pc in plan:
            low, high = max(pr, first), min(pr + n, first + count)
            if low < high:
                jobs.append((index, rel, low - first, pc, a, r + low - pr, c, high - low, w))

    def body(place_ref, *refs):
        sources = refs[: len(arrays)]
        outs = refs[len(arrays) : len(arrays) + len(shapes)]
        sems = refs[-1]
        here = place_ref[0]
        copies = []
        for i, (index, rel, sr, sc, a, r, c, n, w) in enumerate(jobs):
            block = lax.rem(here + rel, RING)
            rows = shapes[a][0] // RING
            start = pl.multiple_of(block * rows + r, 32)
            copies.append(
                pltpu.make_async_copy(
                    sources[index].at[pl.ds(sr, n), pl.ds(sc, w)],
                    outs[a].at[pl.ds(start, n), pl.ds(c, w)],
                    sems.at[i],
                )
            )
        run_copies(copies)

    return pl.pallas_call(
        body,
        in_specs=[pl.BlockSpec(memory_space=pltpu.SMEM)] + in_any(len(arrays)),
        out_specs=in_any(len(shapes)),
        out_shape=[jax.ShapeDtypeStruct(shape, jnp.bfloat16) for shape in shapes],
        scratch_shapes=[pltpu.SemaphoreType.DMA((len(jobs),))],
        name="unpack_full",
    )(place, *arrays)


def pack_blocks(place, arrays, plan, cols):
    half = ROWS // 2
    targets = [(0, 0, ROWS), (1, 0, ROWS), (3, 0, ROWS), (2, 0, half), (2, half, half)]
    jobs = []
    for index, (rel, first, count) in enumerate(targets):
        for a, r, n, c, w, pr, pc in plan:
            low, high = max(pr, first), min(pr + n, first + count)
            if low < high:
                jobs.append((index, rel, low - first, pc, a, r + low - pr, c, high - low, w))

    def body(place_ref, *refs):
        sources = refs[: len(arrays)]
        outs = refs[len(arrays) : len(arrays) + len(targets)]
        sems = refs[-1]
        here = place_ref[0]
        copies = []
        for i, (index, rel, sr, sc, a, r, c, n, w) in enumerate(jobs):
            block = lax.rem(here + rel, RING)
            rows = arrays[a].shape[0] // RING
            start = pl.multiple_of(block * rows + r, 32)
            copies.append(
                pltpu.make_async_copy(
                    sources[a].at[pl.ds(start, n), pl.ds(c, w)],
                    outs[index].at[pl.ds(sr, n), pl.ds(sc, w)],
                    sems.at[i],
                )
            )
        run_copies(copies)

    return pl.pallas_call(
        body,
        in_specs=[pl.BlockSpec(memory_space=pltpu.SMEM)] + in_any(len(arrays)),
        out_specs=in_any(len(targets)),
        out_shape=[jax.ShapeDtypeStruct((t[2], cols), jnp.bfloat16) for t in targets],
        scratch_shapes=[pltpu.SemaphoreType.DMA((len(jobs),))],
        name="pack_blocks",
    )(place, *arrays)


def along_z(x, section, by):
    pairs = [(section * RING + i, section * RING + (i + by) % RING) for i in range(RING)]
    return lax.ppermute(x, ("section", "z"), pairs)


def along_seq(x, section, by):
    count = RING * RING
    pairs = [
        (section * count + i, section * count + i + by) for i in range(count) if 0 <= i + by < count
    ]
    return lax.ppermute(x, ("section", "y", "x"), pairs)


def gather_weights(shard, section, place, plan, shapes):
    half = ROWS // 2
    above = along_z(shard, section, -1)
    below = along_z(shard, section, 1)
    first = along_z(below[:half], section, 1)
    second = along_z(above[half:], section, -1)
    pieces = (
        (shard, 0, 0, ROWS),
        (above, 1, 0, ROWS),
        (below, 3, 0, ROWS),
        (first, 2, 0, half),
        (second, 2, half, half),
    )
    return unpack_full(place, pieces, plan, shapes)


def reduce_z(place, section, arrays, plan, cols):
    own, after, before, far_a, far_b = pack_blocks(place, arrays, plan, cols)
    half = ROWS // 2
    got_a = along_z(far_a, section, 1)
    got_b = along_z(far_b, section, -1)
    after = lax.dynamic_update_slice(after, after[:half] + got_a, (0, 0))
    before = lax.dynamic_update_slice(before, before[half:] + got_b, (half, 0))
    left = along_z(after, section, 1)
    right = along_z(before, section, -1)
    return own, left, right


def total_of(parts):
    own, left, right = (item.astype(jnp.float32) for item in parts)
    return own + left + right


def normalize(values, gain):
    return values * lax.rsqrt(jnp.mean(values * values, axis=-1, keepdims=True) + EPSILON) * gain


def product(left, right):
    return jnp.dot(left, right, preferred_element_type=jnp.float32)


def inner_rows(left, right):
    return lax.dot_general(
        left, right, (((0,), (0,)), ((), ())), preferred_element_type=jnp.float32
    ).astype(jnp.bfloat16)


def against(left, right):
    return lax.dot_general(
        left, right, (((1,), (1,)), ((), ())), preferred_element_type=jnp.float32
    )


def turn(values, cosine, sine):
    half = values.shape[-1] // 2
    former = values[..., :half]
    latter = values[..., half:]
    return jnp.concatenate(
        [former * cosine - latter * sine, latter * cosine + former * sine], axis=-1
    )


def batched(spec, left, right):
    return jnp.einsum(spec, left, right, preferred_element_type=jnp.float32)


def forward_layer(inputs, tables, allowed, attn_w, ffn_w, gains, section):
    qkv_w, output_w = attn_w
    gate_up_w, down_w = ffn_w
    pre_g, query_g, key_g, mix_g, ffn_g, out_g = gains
    cosine, sine = tables
    normed = normalize(inputs, pre_g).astype(jnp.bfloat16)
    key_value = product(normed, qkv_w[:, QH * HD :])
    key_raw = key_value[:, :HD]
    values = key_value[:, HD:].astype(jnp.bfloat16)
    key_rot = turn(normalize(key_raw, key_g), cosine, sine).astype(jnp.bfloat16)
    own = jnp.stack([key_rot, values]).reshape(2, MICRO, SHARD, HD)
    pieces = [along_seq(own, section, by) for by in range(HOPS, 0, -1)]
    query_raw = product(normed, qkv_w[:, : QH * HD]).reshape(MICRO, SHARD, QH, HD)
    query_raw = jnp.swapaxes(query_raw, 1, 2)
    query_rot = turn(
        normalize(query_raw, query_g),
        cosine.reshape(MICRO, 1, SHARD, HD // 2),
        sine.reshape(MICRO, 1, SHARD, HD // 2),
    ).astype(jnp.bfloat16)
    joined = jnp.concatenate(pieces + [own], axis=2)
    keys_all, values_all = joined[0], joined[1]
    raw = batched("mhqd,mkd->mhqk", query_rot, keys_all)
    score = jnp.where(allowed[:, None], raw * HD ** (-0.5), -1e30)
    highest = jnp.max(score, axis=-1, keepdims=True)
    expo = jnp.exp(score - highest)
    prob = expo / jnp.sum(expo, axis=-1, keepdims=True)
    mixed = batched("mhqk,mkd->mhqd", prob.astype(jnp.bfloat16), values_all).astype(jnp.bfloat16)
    mixed = jnp.swapaxes(mixed, 1, 2).reshape(TOKENS, QH * HD)
    branch = product(mixed, output_w)
    middle = inputs + normalize(branch, mix_g)
    inner = normalize(middle, ffn_g).astype(jnp.bfloat16)
    gate_up = product(inner, gate_up_w)
    gate_act = gate_up[:, :FF]
    up_act = gate_up[:, FF:]
    hidden = (jax.nn.gelu(gate_act) * up_act).astype(jnp.bfloat16)
    down = product(hidden, down_w)
    result = (middle + normalize(down, out_g)).astype(jnp.bfloat16)
    stored = (
        inputs, normed, query_raw, key_raw, query_rot, keys_all, values_all, prob, mixed, branch,
        middle, inner, gate_act, up_act, hidden, down,
    )
    return result, stored


def norm_back(grad, values, gain):
    scale = lax.rsqrt(jnp.mean(values * values, axis=-1, keepdims=True) + EPSILON)
    unit = values * scale
    weighted = grad * gain
    dv = scale * (weighted - unit * jnp.mean(weighted * unit, axis=-1, keepdims=True))
    return dv, grad * unit


def backward_layer(grad_out, stored, tables, attn_w, ffn_w, gains, section, place, merge):
    (
        inputs, normed, query_raw, key_raw, query_rot, keys_all, values_all, prob, mixed, branch,
        middle, inner, gate_act, up_act, hidden, down,
    ) = stored
    qkv_w, output_w = attn_w
    gate_up_w, down_w = ffn_w
    pre_g, query_g, key_g, mix_g, ffn_g, out_g = gains
    cosine, sine = tables
    d_down, by_out = norm_back(grad_out, down, out_g)
    d_out_g = jnp.sum(by_out, axis=0)
    d_down = d_down.astype(jnp.bfloat16)
    d_hidden = against(d_down, down_w)
    _, pull = jax.vjp(
        lambda gate_in, up_in: jax.nn.gelu(gate_in) * up_in, gate_act, up_act
    )
    d_gate, d_up = pull(d_hidden)
    d_gate_up = jnp.concatenate([d_gate.astype(jnp.bfloat16), d_up.astype(jnp.bfloat16)], axis=1)
    d_inner = against(d_gate_up, gate_up_w)
    d_middle_ffn, by_ffn = norm_back(d_inner, middle, ffn_g)
    d_ffn_g = jnp.sum(by_ffn, axis=0)
    d_middle = grad_out + d_middle_ffn
    d_branch, by_mix = norm_back(d_middle, branch, mix_g)
    d_mix_g = jnp.sum(by_mix, axis=0)
    d_branch = d_branch.astype(jnp.bfloat16)
    d_mixed = against(d_branch, output_w).astype(jnp.bfloat16).reshape(MICRO, SHARD, QH, HD)
    d_mixed = jnp.swapaxes(d_mixed, 1, 2)
    d_prob = batched("mhqd,mkd->mhqk", d_mixed, values_all)
    d_score = (prob * (d_prob - jnp.sum(prob * d_prob, axis=-1, keepdims=True))).astype(
        jnp.bfloat16
    )
    scale = HD ** (-0.5)
    d_keys = batched("mhqk,mhqd->mkd", d_score, query_rot) * scale
    d_values_all = batched("mhqk,mhqd->mkd", prob.astype(jnp.bfloat16), d_mixed)
    d_stacked = jnp.stack([d_keys, d_values_all])
    back = d_stacked[:, :, HOPS * SHARD :]
    for offset in range(HOPS):
        piece = d_stacked[:, :, offset * SHARD : (offset + 1) * SHARD].astype(jnp.bfloat16)
        back = back + along_seq(piece, section, offset - HOPS).astype(jnp.float32)
    back = back.reshape(2, TOKENS, HD)
    grad_ffn = (inner_rows(inner, d_gate_up), inner_rows(hidden, d_down))
    ffn_parts = None if merge else reduce_z(place, section, grad_ffn, FFN_GRAD_PLAN, FFN_COLS)
    d_query_rot = batched("mhqk,mkd->mhqd", d_score, keys_all) * scale
    d_query, by_query = norm_back(
        turn(
            d_query_rot,
            cosine.reshape(MICRO, 1, SHARD, HD // 2),
            -sine.reshape(MICRO, 1, SHARD, HD // 2),
        ),
        query_raw,
        query_g,
    )
    d_query_g = jnp.sum(by_query, axis=(0, 1, 2))
    d_query = jnp.swapaxes(d_query.astype(jnp.bfloat16), 1, 2).reshape(TOKENS, QH * HD)
    d_values = back[1].astype(jnp.bfloat16)
    d_key, by_key = norm_back(turn(back[0], cosine, -sine), key_raw, key_g)
    d_key_g = jnp.sum(by_key, axis=0)
    d_qkv = jnp.concatenate([d_query, d_key.astype(jnp.bfloat16), d_values], axis=1)
    d_normed = against(d_qkv, qkv_w)
    d_inputs_pre, by_pre = norm_back(d_normed, inputs, pre_g)
    d_pre_g = jnp.sum(by_pre, axis=0)
    d_inputs = d_middle + d_inputs_pre
    grad_attn = (inner_rows(normed, d_qkv), inner_rows(mixed, d_branch))
    gain_grads = jnp.concatenate([d_pre_g, d_query_g, d_key_g, d_mix_g, d_ffn_g, d_out_g])
    return d_inputs, grad_ffn, ffn_parts, grad_attn, gain_grads


GAIN_SIZES = (D, HD, HD, D, D, D)


def per_device(
    hidden_in, positions, segments, cotangent,
    query_weight, key_weight, value_weight, output_weight, gate_weight, up_weight, down_weight,
    pre_gain, query_gain, key_gain, mix_gain, ffn_gain, out_gain,
):
    leading = lax.axis_index("section") == 0
    z_index = lax.axis_index("z")
    seq_index = lax.axis_index("y") * RING + lax.axis_index("x")
    place = jnp.reshape(z_index, (1,)).astype(jnp.int32)

    attn_shard = pack_shard(
        (query_weight[0], key_weight[0], value_weight[0], output_weight[0]), ATTN_PLAN, ATTN_COLS
    )
    ffn_shard = pack_shard((gate_weight[0], up_weight[0], down_weight[0]), FFN_PLAN, FFN_COLS)
    full_attn_plan = ATTN_GRAD_PLAN
    full_ffn_plan = FFN_GRAD_PLAN
    attn_shapes = ((D, QH * HD + 2 * HD), (QH * HD, D))
    ffn_shapes = ((D, 2 * FF), (FF, D))
    weights = []
    for section in range(2):
        attn = gather_weights(attn_shard, section, place, full_attn_plan, attn_shapes)
        ffn = gather_weights(ffn_shard, section, place, full_ffn_plan, ffn_shapes)
        weights.append((attn, ffn))

    packed_gains = jnp.concatenate(
        [item[0] for item in (pre_gain, query_gain, key_gain, mix_gain, ffn_gain, out_gain)]
    )
    all_gains = lax.all_gather(packed_gains, "z").astype(jnp.float32)
    gains = []
    start = 0
    for size in GAIN_SIZES:
        part = size // RING
        gains.append(all_gains[:, start : start + part].reshape(size))
        start += part

    exponent = jnp.arange(HD // 2).astype(jnp.float32) * (2.0 / HD)
    freqs = ROPE_BASE ** (-exponent)
    angle = positions[:, 0].reshape(TOKENS).astype(jnp.float32)[:, None] * freqs[None, :]
    tables = (jnp.cos(angle), jnp.sin(angle))

    segment_rows = segments[:, 0]
    anchor = seq_index * SHARD
    padded = jnp.concatenate([jnp.full((MICRO, WINDOW), -1, jnp.int32), segment_rows], axis=1)
    query_seg = lax.dynamic_slice_in_dim(segment_rows, anchor, SHARD, 1)
    key_seg = lax.dynamic_slice_in_dim(padded, anchor, KEYS, 1)
    gap = (jnp.arange(SHARD, dtype=jnp.int32) + WINDOW)[:, None] - jnp.arange(
        KEYS, dtype=jnp.int32
    )[None, :]
    allowed = (gap >= 0) & (gap < WINDOW)
    allowed = allowed[None] & (query_seg[:, :, None] == key_seg[:, None, :])

    first_in = hidden_in[:, 0].reshape(TOKENS, D).astype(jnp.float32)
    first_out, first_kept = forward_layer(first_in, tables, allowed, *weights[0], gains, 0)
    handed = lax.ppermute(first_out, "section", [(0, 1)]).astype(jnp.float32)
    second_out, second_kept = forward_layer(handed, tables, allowed, *weights[1], gains, 1)

    cot = cotangent[:, 0].reshape(TOKENS, D).astype(jnp.float32)
    d_second, ffn_grad1, _, attn_grad1, gain_grad1 = backward_layer(
        cot, second_kept, tables, *weights[1], gains, 1, place, True
    )
    d_first_out = lax.ppermute(d_second.astype(jnp.bfloat16), "section", [(1, 0)])
    ffn_parts1 = reduce_z(place, 1, ffn_grad1, FFN_GRAD_PLAN, FFN_COLS)
    attn_parts1 = reduce_z(place, 1, attn_grad1, ATTN_GRAD_PLAN, ATTN_COLS)
    d_first, _, ffn_parts0, attn_grad0, gain_grad0 = backward_layer(
        d_first_out.astype(jnp.float32), first_kept, tables, *weights[0], gains, 0, place, False
    )
    attn_parts0 = reduce_z(place, 0, attn_grad0, ATTN_GRAD_PLAN, ATTN_COLS)

    def finish(parts0, parts1, cols):
        mine = jnp.where(leading, total_of(parts0), total_of(parts1)).astype(jnp.bfloat16)
        count = RING * RING
        split = mine.reshape(count, ROWS // count, cols)
        moved = lax.all_to_all(split, ("y", "x"), split_axis=0, concat_axis=0, tiled=True)
        summed = jnp.sum(moved.astype(jnp.float32), axis=0).astype(jnp.bfloat16)
        return lax.all_gather(summed, ("y", "x"), axis=0, tiled=True)

    ffn_done = finish(ffn_parts0, ffn_parts1, FFN_COLS)
    attn_done = finish(attn_parts0, attn_parts1, ATTN_COLS)
    gain_total = lax.psum(jnp.where(leading, gain_grad0, gain_grad1), ("y", "x", "z"))

    def restore(packed, plan, which):
        return jnp.concatenate(
            [packed[pr : pr + n, pc : pc + w] for a, r, n, c, w, pr, pc in plan if a == which]
        ).astype(jnp.float32)[None]

    gain_outs = []
    start = 0
    for size in GAIN_SIZES:
        part = size // RING
        gain_outs.append(lax.dynamic_slice(gain_total, (start + z_index * part,), (part,))[None])
        start += size
    outputs = jnp.where(leading, first_out, second_out).reshape(1, MICRO, 1, SHARD, D)
    input_grads = jnp.where(leading, d_first, d_second).reshape(1, MICRO, 1, SHARD, D)
    return (
        outputs,
        input_grads,
        restore(attn_done, ATTN_PLAN, 0),
        restore(attn_done, ATTN_PLAN, 1),
        restore(attn_done, ATTN_PLAN, 2),
        restore(attn_done, ATTN_PLAN, 3),
        restore(ffn_done, FFN_PLAN, 0),
        restore(ffn_done, FFN_PLAN, 1),
        restore(ffn_done, FFN_PLAN, 2),
    ) + tuple(gain_outs)


def solution(mesh):
    grid = Mesh(
        mesh.devices.reshape(2, RING, RING, RING), ("section", "y", "x", "z")
    )
    seq = ("y", "x")
    in_specs = (
        P(None, "z", seq, None),
        P(None, "z", seq),
        P(None, "z", None),
        P(None, "z", seq, None),
    ) + (P("section", "z", None),) * 7 + (P("section", "z"),) * 6
    out_specs = (
        (P("section", None, "z", seq, None),) * 2
        + (P("section", "z", None),) * 7
        + (P("section", "z"),) * 6
    )
    return jax.shard_map(
        per_device, mesh=grid, in_specs=in_specs, out_specs=out_specs, check_vma=False
    )
```

```python
import jax
import jax.numpy as jnp
import numpy as np
from jax import lax
from jax.experimental import pallas as pl
from jax.experimental.pallas import tpu as pltpu
from jax.sharding import Mesh, PartitionSpec as P

WINDOW = 512
EPSILON = 1e-06
ROPE_BASE = 10000.0

RING = 4
D = 640
FF = 2048
QH = 4
HD = 256
MICRO = 3
SHARD = 128
TOKENS = MICRO * SHARD
HOPS = WINDOW // SHARD
KEYS = SHARD + WINDOW

ROWS = 256
FFN_COLS = 4096
ATTN_COLS = 1920

FFN_PLAN = ((0, 0, 160, 0, 2048, 0, 0), (1, 0, 160, 0, 2048, 0, 2048)) + tuple(
    (2, 96 * i, min(96, 512 - 96 * i), 0, 640, 160, 640 * i) for i in range(6)
)
ATTN_PLAN = (
    (0, 0, 160, 0, 1024, 0, 0),
    (1, 0, 160, 0, 256, 0, 1024),
    (2, 0, 160, 0, 256, 0, 1280),
) + tuple((3, 96 * i, min(96, 256 - 96 * i), 0, 640, 160, 640 * i) for i in range(3)) + (
    (4, 0, 32, 0, 640, 224, 1280),
)

FFN_GRAD_PLAN = ((0, 0, 160, 0, 4096, 0, 0),) + tuple(
    (1, 96 * i, min(96, 512 - 96 * i), 0, 640, 160, 640 * i) for i in range(6)
)
ATTN_GRAD_PLAN = (
    ((0, 0, 160, 0, 1536, 0, 0),)
    + tuple((1, 96 * i, min(96, 256 - 96 * i), 0, 640, 160, 640 * i) for i in range(3))
    + ((2, 0, 32, 0, 640, 224, 1280),)
)


def in_any(count):
    return [pl.BlockSpec(memory_space=pl.ANY)] * count


def in_vmem(count):
    return [pl.BlockSpec(memory_space=pltpu.VMEM)] * count


LIMIT = 24 * 1024 * 1024


def run_copies(copies):
    for item in copies:
        item.start()
    for item in copies:
        item.wait()


def pack_shard(arrays, plan, cols, after=()):
    def body(*refs):
        sources, out, sems = refs[: len(arrays)], refs[-2], refs[-1]
        run_copies(
            [
                pltpu.make_async_copy(
                    sources[a].at[pl.ds(r, n), pl.ds(c, w)],
                    out.at[pl.ds(pr, n), pl.ds(pc, w)],
                    sems.at[i],
                )
                for i, (a, r, n, c, w, pr, pc) in enumerate(plan)
            ]
        )

    return pl.pallas_call(
        body,
        in_specs=in_any(len(arrays) + len(after)),
        out_specs=pl.BlockSpec(memory_space=pltpu.VMEM),
        out_shape=jax.ShapeDtypeStruct((ROWS, cols), jnp.bfloat16),
        compiler_params=pltpu.CompilerParams(vmem_limit_bytes=LIMIT),
        scratch_shapes=[pltpu.SemaphoreType.DMA((len(plan),))],
        name="pack_shard",
    )(*arrays, *after)


def ordered(value, *after):
    return pl.pallas_call(
        lambda *refs: None,
        in_specs=in_any(1 + len(after)),
        out_specs=pl.BlockSpec(memory_space=pl.ANY),
        out_shape=jax.ShapeDtypeStruct(value.shape, value.dtype),
        input_output_aliases={0: 0},
        name="ordered",
    )(value, *after)


def unpack_full(place, pieces, plan, shapes):
    arrays = [item[0] for item in pieces]
    jobs = []
    for index, (_, rel, first, count) in enumerate(pieces):
        for a, r, n, c, w, pr, pc in plan:
            low, high = max(pr, first), min(pr + n, first + count)
            if low < high:
                jobs.append((index, rel, low - first, pc, a, r + low - pr, c, high - low, w))

    def body(place_ref, *refs):
        sources = refs[: len(arrays)]
        outs = refs[len(arrays) : len(arrays) + len(shapes)]
        sems = refs[-1]
        here = place_ref[0]
        copies = []
        for i, (index, rel, sr, sc, a, r, c, n, w) in enumerate(jobs):
            block = lax.rem(here + rel, RING)
            rows = shapes[a][0] // RING
            start = pl.multiple_of(block * rows + r, 32)
            copies.append(
                pltpu.make_async_copy(
                    sources[index].at[pl.ds(sr, n), pl.ds(sc, w)],
                    outs[a].at[pl.ds(start, n), pl.ds(c, w)],
                    sems.at[i],
                )
            )
        run_copies(copies)

    return pl.pallas_call(
        body,
        in_specs=[pl.BlockSpec(memory_space=pltpu.SMEM)] + in_any(len(arrays)),
        out_specs=in_vmem(len(shapes)),
        compiler_params=pltpu.CompilerParams(vmem_limit_bytes=LIMIT),
        out_shape=[jax.ShapeDtypeStruct(shape, jnp.bfloat16) for shape in shapes],
        scratch_shapes=[pltpu.SemaphoreType.DMA((len(jobs),))],
        name="unpack_full",
    )(place, *arrays)


def pack_blocks(place, arrays, plan, cols):
    half = ROWS // 2
    targets = [(0, 0, ROWS), (1, 0, ROWS), (3, 0, ROWS), (2, 0, half), (2, half, half)]
    jobs = []
    for index, (rel, first, count) in enumerate(targets):
        for a, r, n, c, w, pr, pc in plan:
            low, high = max(pr, first), min(pr + n, first + count)
            if low < high:
                jobs.append((index, rel, low - first, pc, a, r + low - pr, c, high - low, w))

    def body(place_ref, *refs):
        sources = refs[: len(arrays)]
        outs = refs[len(arrays) : len(arrays) + len(targets)]
        sems = refs[-1]
        here = place_ref[0]
        copies = []
        for i, (index, rel, sr, sc, a, r, c, n, w) in enumerate(jobs):
            block = lax.rem(here + rel, RING)
            rows = arrays[a].shape[0] // RING
            start = pl.multiple_of(block * rows + r, 32)
            copies.append(
                pltpu.make_async_copy(
                    sources[a].at[pl.ds(start, n), pl.ds(c, w)],
                    outs[index].at[pl.ds(sr, n), pl.ds(sc, w)],
                    sems.at[i],
                )
            )
        run_copies(copies)

    return pl.pallas_call(
        body,
        in_specs=[pl.BlockSpec(memory_space=pltpu.SMEM)] + in_any(len(arrays)),
        out_specs=in_vmem(len(targets)),
        compiler_params=pltpu.CompilerParams(vmem_limit_bytes=LIMIT),
        out_shape=[jax.ShapeDtypeStruct((t[2], cols), jnp.bfloat16) for t in targets],
        scratch_shapes=[pltpu.SemaphoreType.DMA((len(jobs),))],
        name="pack_blocks",
    )(place, *arrays)


def along_z(x, section, by):
    pairs = [(section * RING + i, section * RING + (i + by) % RING) for i in range(RING)]
    return lax.ppermute(x, ("section", "z"), pairs)


def along_seq(x, section, by):
    count = RING * RING
    pairs = [
        (section * count + i, section * count + i + by) for i in range(count) if 0 <= i + by < count
    ]
    return lax.ppermute(x, ("section", "y", "x"), pairs)


def gather_weights(shard, section, place, plan, shapes):
    half = ROWS // 2
    above = along_z(shard, section, -1)
    below = along_z(shard, section, 1)
    first = along_z(below[:half], section, 1)
    second = along_z(above[half:], section, -1)
    pieces = (
        (shard, 0, 0, ROWS),
        (above, 1, 0, ROWS),
        (below, 3, 0, ROWS),
        (first, 2, 0, half),
        (second, 2, half, half),
    )
    return unpack_full(place, pieces, plan, shapes), (above, below)


def reduce_z_begin(place, section, arrays, plan, cols):
    own, after, before, far_a, far_b = pack_blocks(place, arrays, plan, cols)
    return own, after, before, along_z(far_a, section, 1), along_z(far_b, section, -1)


def reduce_z_end(begun, section):
    own, after, before, got_a, got_b = begun
    half = ROWS // 2
    after = lax.dynamic_update_slice(after, after[:half] + got_a, (0, 0))
    before = lax.dynamic_update_slice(before, before[half:] + got_b, (half, 0))
    return own, along_z(after, section, 1), along_z(before, section, -1)


def total_of(parts):
    own, left, right = (item.astype(jnp.float32) for item in parts)
    return own + left + right


def normalize(values, gain):
    return values * lax.rsqrt(jnp.mean(values * values, axis=-1, keepdims=True) + EPSILON) * gain


def product(left, right):
    return jnp.dot(left, right, preferred_element_type=jnp.float32)


def inner_rows(left, right):
    return lax.dot_general(
        left, right, (((0,), (0,)), ((), ())), preferred_element_type=jnp.float32
    ).astype(jnp.bfloat16)


def against(left, right):
    return lax.dot_general(
        left, right, (((1,), (1,)), ((), ())), preferred_element_type=jnp.float32
    )


def turn(values, cosine, sine):
    half = values.shape[-1] // 2
    former = values[..., :half]
    latter = values[..., half:]
    return jnp.concatenate(
        [former * cosine - latter * sine, latter * cosine + former * sine], axis=-1
    )


def batched(spec, left, right):
    return jnp.einsum(spec, left, right, preferred_element_type=jnp.float32)


def forward_layer(inputs, tables, allowed, attn_w, ffn_w, gains, section):
    qkv_w, output_w = attn_w
    gate_up_w, down_w = ffn_w
    pre_g, query_g, key_g, mix_g, ffn_g, out_g = gains
    cosine, sine = tables
    normed = normalize(inputs, pre_g).astype(jnp.bfloat16)
    key_value = product(normed, qkv_w[:, QH * HD :])
    key_raw = key_value[:, :HD]
    values = key_value[:, HD:].astype(jnp.bfloat16)
    key_rot = turn(normalize(key_raw, key_g), cosine, sine).astype(jnp.bfloat16)
    own = jnp.stack([key_rot, values]).reshape(2, MICRO, SHARD, HD)
    pieces = [along_seq(own, section, by) for by in range(HOPS, 0, -1)]
    query_raw = product(normed, qkv_w[:, : QH * HD]).reshape(MICRO, SHARD, QH, HD)
    query_raw = jnp.swapaxes(query_raw, 1, 2)
    query_rot = turn(
        normalize(query_raw, query_g),
        cosine.reshape(MICRO, 1, SHARD, HD // 2),
        sine.reshape(MICRO, 1, SHARD, HD // 2),
    ).astype(jnp.bfloat16)
    joined = jnp.concatenate(pieces + [own], axis=2)
    keys_all, values_all = joined[0], joined[1]
    raw = batched("mhqd,mkd->mhqk", query_rot, keys_all)
    score = jnp.where(allowed[:, None], raw * HD ** (-0.5), -1e30)
    highest = jnp.max(score, axis=-1, keepdims=True)
    expo = jnp.exp(score - highest)
    prob = expo / jnp.sum(expo, axis=-1, keepdims=True)
    mixed = batched("mhqk,mkd->mhqd", prob.astype(jnp.bfloat16), values_all).astype(jnp.bfloat16)
    mixed = jnp.swapaxes(mixed, 1, 2).reshape(TOKENS, QH * HD)
    branch = product(mixed, output_w)
    middle = inputs + normalize(branch, mix_g)
    inner = normalize(middle, ffn_g).astype(jnp.bfloat16)
    gate_up = product(inner, gate_up_w)
    gate_act = gate_up[:, :FF]
    up_act = gate_up[:, FF:]
    hidden = (jax.nn.gelu(gate_act) * up_act).astype(jnp.bfloat16)
    down = product(hidden, down_w)
    result = (middle + normalize(down, out_g)).astype(jnp.bfloat16)
    stored = (
        inputs, normed, query_raw, key_raw, query_rot, keys_all, values_all, prob, mixed, branch,
        middle, inner, gate_act, up_act, hidden, down,
    )
    return result, stored


def norm_back(grad, values, gain):
    scale = lax.rsqrt(jnp.mean(values * values, axis=-1, keepdims=True) + EPSILON)
    unit = values * scale
    weighted = grad * gain
    dv = scale * (weighted - unit * jnp.mean(weighted * unit, axis=-1, keepdims=True))
    return dv, grad * unit


def backward_layer(
    grad_out, stored, tables, attn_w, ffn_w, gains, section, place, other_ffn=None, other_attn=None
):
    (
        inputs, normed, query_raw, key_raw, query_rot, keys_all, values_all, prob, mixed, branch,
        middle, inner, gate_act, up_act, hidden, down,
    ) = stored
    qkv_w, output_w = attn_w
    gate_up_w, down_w = ffn_w
    pre_g, query_g, key_g, mix_g, ffn_g, out_g = gains
    cosine, sine = tables
    d_down, by_out = norm_back(grad_out, down, out_g)
    d_out_g = jnp.sum(by_out, axis=0)
    d_down = d_down.astype(jnp.bfloat16)
    d_hidden = against(d_down, down_w)
    _, pull = jax.vjp(
        lambda gate_in, up_in: jax.nn.gelu(gate_in) * up_in, gate_act, up_act
    )
    d_gate, d_up = pull(d_hidden)
    d_gate_up = jnp.concatenate([d_gate.astype(jnp.bfloat16), d_up.astype(jnp.bfloat16)], axis=1)
    grad_ffn = (inner_rows(inner, d_gate_up), inner_rows(hidden, d_down))
    ffn_begun = reduce_z_begin(place, section, grad_ffn, FFN_GRAD_PLAN, FFN_COLS)
    if other_ffn is not None:
        d_gate_up = ordered(d_gate_up, *other_ffn[1:])
    d_inner = against(d_gate_up, gate_up_w)
    d_middle_ffn, by_ffn = norm_back(d_inner, middle, ffn_g)
    d_ffn_g = jnp.sum(by_ffn, axis=0)
    d_middle = grad_out + d_middle_ffn
    d_branch, by_mix = norm_back(d_middle, branch, mix_g)
    d_mix_g = jnp.sum(by_mix, axis=0)
    d_branch = d_branch.astype(jnp.bfloat16)
    if other_attn is not None:
        d_branch = ordered(d_branch, *other_attn[1:])
    d_mixed = against(d_branch, output_w).astype(jnp.bfloat16).reshape(MICRO, SHARD, QH, HD)
    d_mixed = jnp.swapaxes(d_mixed, 1, 2)
    d_prob = batched("mhqd,mkd->mhqk", d_mixed, values_all)
    d_score = (prob * (d_prob - jnp.sum(prob * d_prob, axis=-1, keepdims=True))).astype(
        jnp.bfloat16
    )
    d_score = ordered(d_score, ffn_begun[3], ffn_begun[4])
    ffn_parts = reduce_z_end(ffn_begun, section)
    scale = HD ** (-0.5)
    d_keys = batched("mhqk,mhqd->mkd", d_score, query_rot) * scale
    d_values_all = batched("mhqk,mhqd->mkd", prob.astype(jnp.bfloat16), d_mixed)
    d_stacked = jnp.stack([d_keys, d_values_all])
    back = d_stacked[:, :, HOPS * SHARD :]
    for offset in range(HOPS):
        piece = d_stacked[:, :, offset * SHARD : (offset + 1) * SHARD].astype(jnp.bfloat16)
        back = back + along_seq(piece, section, offset - HOPS).astype(jnp.float32)
    back = back.reshape(2, TOKENS, HD)
    d_query_rot = batched("mhqk,mkd->mhqd", d_score, keys_all) * scale
    d_query, by_query = norm_back(
        turn(
            d_query_rot,
            cosine.reshape(MICRO, 1, SHARD, HD // 2),
            -sine.reshape(MICRO, 1, SHARD, HD // 2),
        ),
        query_raw,
        query_g,
    )
    d_query_g = jnp.sum(by_query, axis=(0, 1, 2))
    d_query = jnp.swapaxes(d_query.astype(jnp.bfloat16), 1, 2).reshape(TOKENS, QH * HD)
    d_values = back[1].astype(jnp.bfloat16)
    d_key, by_key = norm_back(turn(back[0], cosine, -sine), key_raw, key_g)
    d_key_g = jnp.sum(by_key, axis=0)
    d_qkv = jnp.concatenate([d_query, d_key.astype(jnp.bfloat16), d_values], axis=1)
    d_normed = against(d_qkv, qkv_w)
    d_inputs_pre, by_pre = norm_back(d_normed, inputs, pre_g)
    d_pre_g = jnp.sum(by_pre, axis=0)
    d_inputs = d_middle + d_inputs_pre
    wide = jnp.stack([d_pre_g, d_mix_g, d_ffn_g, d_out_g]).reshape(4, RING, D // RING)
    narrow = jnp.stack([d_query_g, d_key_g]).reshape(2, RING, HD // RING)
    rows = jnp.concatenate(
        [
            jnp.pad(jnp.swapaxes(wide, 0, 1), ((0, 0), (0, 0), (0, D - D // RING))),
            jnp.pad(jnp.swapaxes(narrow, 0, 1), ((0, 0), (0, 26), (0, D - HD // RING))),
        ],
        axis=1,
    ).astype(jnp.bfloat16)
    grad_attn = (
        inner_rows(normed, d_qkv),
        inner_rows(mixed, d_branch),
        rows.reshape(RING * 32, D),
    )
    return d_inputs, ffn_parts, grad_attn


GAIN_SIZES = (D, HD, HD, D, D, D)
GAIN_ROWS = (0, 4, 5, 1, 2, 3)


def per_device(
    hidden_in, positions, segments, cotangent,
    query_weight, key_weight, value_weight, output_weight, gate_weight, up_weight, down_weight,
    pre_gain, query_gain, key_gain, mix_gain, ffn_gain, out_gain,
):
    leading = lax.axis_index("section") == 0
    z_index = lax.axis_index("z")
    seq_index = lax.axis_index("y") * RING + lax.axis_index("x")
    place = jnp.reshape(z_index, (1,)).astype(jnp.int32)

    wide = jnp.concatenate([pre_gain, mix_gain, ffn_gain, out_gain])
    narrow = jnp.concatenate([query_gain, key_gain])
    gain_shard = jnp.concatenate(
        [
            jnp.pad(wide, ((0, 0), (0, D - D // RING))),
            jnp.pad(narrow, ((0, 26), (0, D - HD // RING))),
        ]
    )
    attn_arrays = (query_weight[0], key_weight[0], value_weight[0], output_weight[0], gain_shard)
    ffn_arrays = (gate_weight[0], up_weight[0], down_weight[0])
    attn_shapes = ((D, QH * HD + 2 * HD), (QH * HD, D), (RING * 32, D))
    ffn_shapes = ((D, 2 * FF), (FF, D))
    weights = []
    gains = []
    seen = ()
    for section in range(2):
        shard = pack_shard(attn_arrays, ATTN_PLAN, ATTN_COLS, seen)
        attn, seen = gather_weights(shard, section, place, ATTN_GRAD_PLAN, attn_shapes)
        shard = pack_shard(ffn_arrays, FFN_PLAN, FFN_COLS, seen)
        ffn, seen = gather_weights(shard, section, place, FFN_GRAD_PLAN, ffn_shapes)
        weights.append((attn[:2], ffn))
        corner = attn[2].reshape(RING, 32, D).astype(jnp.float32)
        gains.append(
            [
                corner[:, row, : size // RING].reshape(size)
                for row, size in zip(GAIN_ROWS, GAIN_SIZES)
            ]
        )

    exponent = jnp.arange(HD // 2).astype(jnp.float32) * (2.0 / HD)
    freqs = ROPE_BASE ** (-exponent)
    angle = positions[:, 0].reshape(TOKENS).astype(jnp.float32)[:, None] * freqs[None, :]
    tables = (jnp.cos(angle), jnp.sin(angle))

    segment_rows = segments[:, 0]
    anchor = seq_index * SHARD
    padded = jnp.concatenate([jnp.full((MICRO, WINDOW), -1, jnp.int32), segment_rows], axis=1)
    query_seg = lax.dynamic_slice_in_dim(segment_rows, anchor, SHARD, 1)
    key_seg = lax.dynamic_slice_in_dim(padded, anchor, KEYS, 1)
    gap = (jnp.arange(SHARD, dtype=jnp.int32) + WINDOW)[:, None] - jnp.arange(
        KEYS, dtype=jnp.int32
    )[None, :]
    allowed = (gap >= 0) & (gap < WINDOW)
    allowed = allowed[None] & (query_seg[:, :, None] == key_seg[:, None, :])

    first_in = hidden_in[:, 0].reshape(TOKENS, D).astype(jnp.float32)
    first_out, first_kept = forward_layer(first_in, tables, allowed, *weights[0], gains[0], 0)
    handed = lax.ppermute(first_out, "section", [(0, 1)]).astype(jnp.float32)
    second_out, second_kept = forward_layer(handed, tables, allowed, *weights[1], gains[1], 1)

    cot = cotangent[:, 0].reshape(TOKENS, D).astype(jnp.float32)
    d_second, ffn_parts1, attn_grad1 = backward_layer(
        cot, second_kept, tables, *weights[1], gains[1], 1, place
    )
    d_first_out = lax.ppermute(d_second.astype(jnp.bfloat16), "section", [(1, 0)])
    attn_parts1 = reduce_z_end(
        reduce_z_begin(place, 1, attn_grad1, ATTN_GRAD_PLAN, ATTN_COLS), 1
    )
    d_first, ffn_parts0, attn_grad0 = backward_layer(
        d_first_out.astype(jnp.float32), first_kept, tables, *weights[0], gains[0], 0, place,
        ffn_parts1, attn_parts1,
    )
    attn_parts0 = reduce_z_end(
        reduce_z_begin(place, 0, attn_grad0, ATTN_GRAD_PLAN, ATTN_COLS), 0
    )

    def finish(parts0, parts1, cols):
        mine = jnp.where(leading, total_of(parts0), total_of(parts1)).astype(jnp.bfloat16)
        count = RING * RING
        split = mine.reshape(count, ROWS // count, cols)
        moved = lax.all_to_all(split, ("y", "x"), split_axis=0, concat_axis=0, tiled=True)
        summed = jnp.sum(moved.astype(jnp.float32), axis=0).astype(jnp.bfloat16)
        return lax.all_gather(summed, ("y", "x"), axis=0, tiled=True)

    ffn_done = finish(ffn_parts0, ffn_parts1, FFN_COLS)
    attn_done = finish(attn_parts0, attn_parts1, ATTN_COLS)

    def restore(packed, plan, which):
        return jnp.concatenate(
            [packed[pr : pr + n, pc : pc + w] for a, r, n, c, w, pr, pc in plan if a == which]
        ).astype(jnp.float32)[None]

    corner = attn_done[224:256, 1280:1920].astype(jnp.float32)
    gain_outs = [
        corner[row : row + 1, : size // RING] for row, size in zip(GAIN_ROWS, GAIN_SIZES)
    ]
    outputs = jnp.where(leading, first_out, second_out).reshape(1, MICRO, 1, SHARD, D)
    input_grads = jnp.where(leading, d_first, d_second).reshape(1, MICRO, 1, SHARD, D)
    return (
        outputs,
        input_grads,
        restore(attn_done, ATTN_PLAN, 0),
        restore(attn_done, ATTN_PLAN, 1),
        restore(attn_done, ATTN_PLAN, 2),
        restore(attn_done, ATTN_PLAN, 3),
        restore(ffn_done, FFN_PLAN, 0),
        restore(ffn_done, FFN_PLAN, 1),
        restore(ffn_done, FFN_PLAN, 2),
    ) + tuple(gain_outs)


def solution(mesh):
    grid = Mesh(
        mesh.devices.reshape(2, RING, RING, RING), ("section", "y", "x", "z")
    )
    seq = ("y", "x")
    in_specs = (
        P(None, "z", seq, None),
        P(None, "z", seq),
        P(None, "z", None),
        P(None, "z", seq, None),
    ) + (P("section", "z", None),) * 7 + (P("section", "z"),) * 6
    out_specs = (
        (P("section", None, "z", seq, None),) * 2
        + (P("section", "z", None),) * 7
        + (P("section", "z"),) * 6
    )
    return jax.shard_map(
        per_device, mesh=grid, in_specs=in_specs, out_specs=out_specs, check_vma=False
    )
```

```python
import jax
import jax.numpy as jnp
import numpy as np
from jax import lax
from jax.experimental import pallas as pl
from jax.experimental.pallas import tpu as pltpu
from jax.sharding import Mesh, PartitionSpec as P

WINDOW = 512
EPSILON = 1e-06
ROPE_BASE = 10000.0

RING = 4
D = 640
FF = 2048
QH = 4
HD = 256
MICRO = 3
SHARD = 128
TOKENS = MICRO * SHARD
HOPS = WINDOW // SHARD
KEYS = SHARD + WINDOW

ROWS = 256
FFN_COLS = 4096
ATTN_COLS = 1920

FFN_PLAN = ((0, 0, 160, 0, 2048, 0, 0), (1, 0, 160, 0, 2048, 0, 2048)) + tuple(
    (2, 96 * i, min(96, 512 - 96 * i), 0, 640, 160, 640 * i) for i in range(6)
)
ATTN_PLAN = (
    (0, 0, 160, 0, 1024, 0, 0),
    (1, 0, 160, 0, 256, 0, 1024),
    (2, 0, 160, 0, 256, 0, 1280),
) + tuple((3, 96 * i, min(96, 256 - 96 * i), 0, 640, 160, 640 * i) for i in range(3)) + (
    (4, 0, 32, 0, 640, 224, 1280),
)

FFN_GRAD_PLAN = ((0, 0, 160, 0, 4096, 0, 0),) + tuple(
    (1, 96 * i, min(96, 512 - 96 * i), 0, 640, 160, 640 * i) for i in range(6)
)
ATTN_GRAD_PLAN = (
    ((0, 0, 160, 0, 1536, 0, 0),)
    + tuple((1, 96 * i, min(96, 256 - 96 * i), 0, 640, 160, 640 * i) for i in range(3))
    + ((2, 0, 32, 0, 640, 224, 1280),)
)


def in_any(count):
    return [pl.BlockSpec(memory_space=pl.ANY)] * count


def in_vmem(count):
    return [pl.BlockSpec(memory_space=pltpu.VMEM)] * count


LIMIT = 24 * 1024 * 1024


def run_copies(copies):
    for item in copies:
        item.start()
    for item in copies:
        item.wait()


def pack_shard(arrays, plan, cols, after=()):
    def body(*refs):
        sources, out, sems = refs[: len(arrays)], refs[-2], refs[-1]
        run_copies(
            [
                pltpu.make_async_copy(
                    sources[a].at[pl.ds(r, n), pl.ds(c, w)],
                    out.at[pl.ds(pr, n), pl.ds(pc, w)],
                    sems.at[i],
                )
                for i, (a, r, n, c, w, pr, pc) in enumerate(plan)
            ]
        )

    return pl.pallas_call(
        body,
        in_specs=in_any(len(arrays) + len(after)),
        out_specs=pl.BlockSpec(memory_space=pltpu.VMEM),
        out_shape=jax.ShapeDtypeStruct((ROWS, cols), jnp.bfloat16),
        compiler_params=pltpu.CompilerParams(vmem_limit_bytes=LIMIT),
        scratch_shapes=[pltpu.SemaphoreType.DMA((len(plan),))],
        name="pack_shard",
    )(*arrays, *after)


def ordered(value, *after):
    return pl.pallas_call(
        lambda *refs: None,
        in_specs=in_any(1 + len(after)),
        out_specs=pl.BlockSpec(memory_space=pl.ANY),
        out_shape=jax.ShapeDtypeStruct(value.shape, value.dtype),
        input_output_aliases={0: 0},
        name="ordered",
    )(value, *after)


def unpack_full(place, pieces, plan, shapes, after=()):
    arrays = [item[0] for item in pieces]
    jobs = []
    for index, (_, rel, first, count) in enumerate(pieces):
        for a, r, n, c, w, pr, pc in plan:
            low, high = max(pr, first), min(pr + n, first + count)
            if low < high:
                jobs.append((index, rel, low - first, pc, a, r + low - pr, c, high - low, w))

    def body(place_ref, *refs):
        sources = refs[: len(arrays)]
        outs = refs[-1 - len(shapes) : -1]
        sems = refs[-1]
        here = place_ref[0]
        copies = []
        for i, (index, rel, sr, sc, a, r, c, n, w) in enumerate(jobs):
            block = lax.rem(here + rel, RING)
            rows = shapes[a][0] // RING
            start = pl.multiple_of(block * rows + r, 32)
            copies.append(
                pltpu.make_async_copy(
                    sources[index].at[pl.ds(sr, n), pl.ds(sc, w)],
                    outs[a].at[pl.ds(start, n), pl.ds(c, w)],
                    sems.at[i],
                )
            )
        run_copies(copies)

    return pl.pallas_call(
        body,
        in_specs=[pl.BlockSpec(memory_space=pltpu.SMEM)] + in_any(len(arrays) + len(after)),
        out_specs=in_vmem(len(shapes)),
        compiler_params=pltpu.CompilerParams(vmem_limit_bytes=LIMIT),
        out_shape=[jax.ShapeDtypeStruct(shape, jnp.bfloat16) for shape in shapes],
        scratch_shapes=[pltpu.SemaphoreType.DMA((len(jobs),))],
        name="unpack_full",
    )(place, *arrays, *after)


def pack_blocks(place, arrays, plan, cols):
    half = ROWS // 2
    targets = [(0, 0, ROWS), (1, 0, ROWS), (3, 0, ROWS), (2, 0, half), (2, half, half)]
    jobs = []
    for index, (rel, first, count) in enumerate(targets):
        for a, r, n, c, w, pr, pc in plan:
            low, high = max(pr, first), min(pr + n, first + count)
            if low < high:
                jobs.append((index, rel, low - first, pc, a, r + low - pr, c, high - low, w))

    def body(place_ref, *refs):
        sources = refs[: len(arrays)]
        outs = refs[len(arrays) : len(arrays) + len(targets)]
        sems = refs[-1]
        here = place_ref[0]
        copies = []
        for i, (index, rel, sr, sc, a, r, c, n, w) in enumerate(jobs):
            block = lax.rem(here + rel, RING)
            rows = arrays[a].shape[0] // RING
            start = pl.multiple_of(block * rows + r, 32)
            copies.append(
                pltpu.make_async_copy(
                    sources[a].at[pl.ds(start, n), pl.ds(c, w)],
                    outs[index].at[pl.ds(sr, n), pl.ds(sc, w)],
                    sems.at[i],
                )
            )
        run_copies(copies)

    return pl.pallas_call(
        body,
        in_specs=[pl.BlockSpec(memory_space=pltpu.SMEM)] + in_any(len(arrays)),
        out_specs=in_vmem(len(targets)),
        compiler_params=pltpu.CompilerParams(vmem_limit_bytes=LIMIT),
        out_shape=[jax.ShapeDtypeStruct((t[2], cols), jnp.bfloat16) for t in targets],
        scratch_shapes=[pltpu.SemaphoreType.DMA((len(jobs),))],
        name="pack_blocks",
    )(place, *arrays)


def along_z(x, by):
    return lax.ppermute(x, "z", [(i, (i + by) % RING) for i in range(RING)])


def along_seq(x, section, by):
    count = RING * RING
    pairs = [
        (section * count + i, section * count + i + by) for i in range(count) if 0 <= i + by < count
    ]
    return lax.ppermute(x, ("section", "y", "x"), pairs)


def gather_weights(shard):
    half = ROWS // 2
    above = along_z(shard, -1)
    below = along_z(shard, 1)
    first = along_z(below[:half], 1)
    second = along_z(above[half:], -1)
    return (
        (shard, 0, 0, ROWS),
        (above, 1, 0, ROWS),
        (below, 3, 0, ROWS),
        (first, 2, 0, half),
        (second, 2, half, half),
    )


def reduce_z_begin(place, arrays, plan, cols):
    own, after, before, far_a, far_b = pack_blocks(place, arrays, plan, cols)
    return own, after, before, along_z(far_a, 1), along_z(far_b, -1)


def reduce_z_end(begun):
    own, after, before, got_a, got_b = begun
    half = ROWS // 2
    after = lax.dynamic_update_slice(after, after[:half] + got_a, (0, 0))
    before = lax.dynamic_update_slice(before, before[half:] + got_b, (half, 0))
    return own, along_z(after, 1), along_z(before, -1)


def unpack_grads(packed, plan, shapes):
    def body(source, *outs):
        for a, r, n, c, w, pr, pc in plan:
            outs[a][pl.ds(r, n), pl.ds(c, w)] = source[pl.ds(pr, n), pl.ds(pc, w)].astype(
                jnp.float32
            )

    return pl.pallas_call(
        body,
        in_specs=in_vmem(1),
        out_specs=in_vmem(len(shapes)),
        out_shape=[jax.ShapeDtypeStruct(shape, jnp.float32) for shape in shapes],
        compiler_params=pltpu.CompilerParams(vmem_limit_bytes=LIMIT),
        name="unpack_grads",
    )(packed)


def total_of(parts):
    own, left, right = (item.astype(jnp.float32) for item in parts)
    return own + left + right


def normalize(values, gain):
    return values * lax.rsqrt(jnp.mean(values * values, axis=-1, keepdims=True) + EPSILON) * gain


def product(left, right):
    return jnp.dot(left, right, preferred_element_type=jnp.float32)


def inner_rows(left, right):
    return lax.dot_general(
        left, right, (((0,), (0,)), ((), ())), preferred_element_type=jnp.float32
    ).astype(jnp.bfloat16)


def against(left, right):
    return lax.dot_general(
        left, right, (((1,), (1,)), ((), ())), preferred_element_type=jnp.float32
    )


def turn(values, cosine, sine):
    half = values.shape[-1] // 2
    former = values[..., :half]
    latter = values[..., half:]
    return jnp.concatenate(
        [former * cosine - latter * sine, latter * cosine + former * sine], axis=-1
    )


def batched(spec, left, right):
    return jnp.einsum(spec, left, right, preferred_element_type=jnp.float32)


def forward_layer(inputs, tables, allowed, attn_w, gains, section, ffn_weights):
    qkv_w, output_w = attn_w
    pre_g, query_g, key_g, mix_g, ffn_g, out_g = gains
    cosine, sine = tables
    normed = normalize(inputs, pre_g).astype(jnp.bfloat16)
    key_value = product(normed, qkv_w[:, QH * HD :])
    key_raw = key_value[:, :HD]
    values = key_value[:, HD:].astype(jnp.bfloat16)
    key_rot = turn(normalize(key_raw, key_g), cosine, sine).astype(jnp.bfloat16)
    own = jnp.stack([key_rot, values]).reshape(2, MICRO, SHARD, HD)
    pieces = [along_seq(own, section, by) for by in range(HOPS, 0, -1)]
    query_raw = product(normed, qkv_w[:, : QH * HD]).reshape(MICRO, SHARD, QH, HD)
    query_raw = jnp.swapaxes(query_raw, 1, 2)
    query_rot = turn(
        normalize(query_raw, query_g),
        cosine.reshape(MICRO, 1, SHARD, HD // 2),
        sine.reshape(MICRO, 1, SHARD, HD // 2),
    ).astype(jnp.bfloat16)
    joined = jnp.concatenate(pieces + [own], axis=2)
    keys_all, values_all = joined[0], joined[1]
    raw = batched("mhqd,mkd->mhqk", query_rot, keys_all)
    score = jnp.where(allowed[:, None], raw * HD ** (-0.5), -1e30)
    highest = jnp.max(score, axis=-1, keepdims=True)
    expo = jnp.exp(score - highest)
    prob = expo / jnp.sum(expo, axis=-1, keepdims=True)
    mixed = batched("mhqk,mkd->mhqd", prob.astype(jnp.bfloat16), values_all).astype(jnp.bfloat16)
    mixed = jnp.swapaxes(mixed, 1, 2).reshape(TOKENS, QH * HD)
    mixed, (gate_up_w, down_w) = ffn_weights(mixed)
    branch = product(mixed, output_w)
    middle = inputs + normalize(branch, mix_g)
    inner = normalize(middle, ffn_g).astype(jnp.bfloat16)
    gate_up = product(inner, gate_up_w)
    gate_act = gate_up[:, :FF]
    up_act = gate_up[:, FF:]
    hidden = (jax.nn.gelu(gate_act) * up_act).astype(jnp.bfloat16)
    down = product(hidden, down_w)
    result = (middle + normalize(down, out_g)).astype(jnp.bfloat16)
    stored = (
        inputs, normed, query_raw, key_raw, query_rot, keys_all, values_all, prob, mixed, branch,
        middle, inner, gate_act, up_act, hidden, down,
    )
    return result, stored


ATTN_SHAPES = ((D, QH * HD + 2 * HD), (QH * HD, D), (RING * 32, D))
FFN_SHAPES = ((D, 2 * FF), (FF, D))


def norm_back(grad, values, gain):
    scale = lax.rsqrt(jnp.mean(values * values, axis=-1, keepdims=True) + EPSILON)
    unit = values * scale
    weighted = grad * gain
    dv = scale * (weighted - unit * jnp.mean(weighted * unit, axis=-1, keepdims=True))
    return dv, grad * unit


def backward_layer(
    grad_out, stored, tables, attn_w, ffn_w, gains, section, place=None, leading=None, other=None
):
    def chosen(name, mine):
        return jnp.where(leading, mine, other[name])

    kept = {}
    (
        inputs, normed, query_raw, key_raw, query_rot, keys_all, values_all, prob, mixed, branch,
        middle, inner, gate_act, up_act, hidden, down,
    ) = stored
    qkv_w, output_w = attn_w
    gate_up_w, down_w = ffn_w
    pre_g, query_g, key_g, mix_g, ffn_g, out_g = gains
    cosine, sine = tables
    d_down, by_out = norm_back(grad_out, down, out_g)
    d_out_g = jnp.sum(by_out, axis=0)
    d_down = d_down.astype(jnp.bfloat16)
    d_hidden = against(d_down, down_w)
    _, pull = jax.vjp(
        lambda gate_in, up_in: jax.nn.gelu(gate_in) * up_in, gate_act, up_act
    )
    d_gate, d_up = pull(d_hidden)
    d_gate_up = jnp.concatenate([d_gate.astype(jnp.bfloat16), d_up.astype(jnp.bfloat16)], axis=1)
    kept.update(inner=inner, d_gate_up=d_gate_up, hidden=hidden, d_down=d_down)
    if other is not None:
        picked = {name: chosen(name, kept[name]) for name in kept}
        grad_ffn = (
            inner_rows(picked["inner"], picked["d_gate_up"]),
            inner_rows(picked["hidden"], picked["d_down"]),
        )
        ffn_begun = reduce_z_begin(place, grad_ffn, FFN_GRAD_PLAN, FFN_COLS)
    d_inner = against(d_gate_up, gate_up_w)
    d_middle_ffn, by_ffn = norm_back(d_inner, middle, ffn_g)
    d_ffn_g = jnp.sum(by_ffn, axis=0)
    d_middle = grad_out + d_middle_ffn
    d_branch, by_mix = norm_back(d_middle, branch, mix_g)
    d_mix_g = jnp.sum(by_mix, axis=0)
    d_branch = d_branch.astype(jnp.bfloat16)
    d_mixed = against(d_branch, output_w).astype(jnp.bfloat16)
    if other is not None:
        d_mixed = ordered(d_mixed, ffn_begun[3], ffn_begun[4])
        ffn_parts = reduce_z_end(ffn_begun)
    d_mixed = jnp.swapaxes(d_mixed.reshape(MICRO, SHARD, QH, HD), 1, 2)
    d_prob = batched("mhqd,mkd->mhqk", d_mixed, values_all)
    d_score = (prob * (d_prob - jnp.sum(prob * d_prob, axis=-1, keepdims=True))).astype(
        jnp.bfloat16
    )
    scale = HD ** (-0.5)
    d_keys = batched("mhqk,mhqd->mkd", d_score, query_rot) * scale
    d_values_all = batched("mhqk,mhqd->mkd", prob.astype(jnp.bfloat16), d_mixed)
    d_stacked = jnp.stack([d_keys, d_values_all])
    back = d_stacked[:, :, HOPS * SHARD :]
    for offset in range(HOPS):
        piece = d_stacked[:, :, offset * SHARD : (offset + 1) * SHARD].astype(jnp.bfloat16)
        back = back + along_seq(piece, section, offset - HOPS).astype(jnp.float32)
    back = back.reshape(2, TOKENS, HD)
    d_query_rot = batched("mhqk,mkd->mhqd", d_score, keys_all) * scale
    d_query, by_query = norm_back(
        turn(
            d_query_rot,
            cosine.reshape(MICRO, 1, SHARD, HD // 2),
            -sine.reshape(MICRO, 1, SHARD, HD // 2),
        ),
        query_raw,
        query_g,
    )
    d_query_g = jnp.sum(by_query, axis=(0, 1, 2))
    d_query = jnp.swapaxes(d_query.astype(jnp.bfloat16), 1, 2).reshape(TOKENS, QH * HD)
    d_values = back[1].astype(jnp.bfloat16)
    d_key, by_key = norm_back(turn(back[0], cosine, -sine), key_raw, key_g)
    d_key_g = jnp.sum(by_key, axis=0)
    d_qkv = jnp.concatenate([d_query, d_key.astype(jnp.bfloat16), d_values], axis=1)
    if other is not None:
        d_qkv = ordered(d_qkv, *ffn_parts[1:])
    d_normed = against(d_qkv, qkv_w)
    d_inputs_pre, by_pre = norm_back(d_normed, inputs, pre_g)
    d_pre_g = jnp.sum(by_pre, axis=0)
    d_inputs = d_middle + d_inputs_pre
    wide = jnp.stack([d_pre_g, d_mix_g, d_ffn_g, d_out_g]).reshape(4, RING, D // RING)
    narrow = jnp.stack([d_query_g, d_key_g]).reshape(2, RING, HD // RING)
    rows = jnp.concatenate(
        [
            jnp.pad(jnp.swapaxes(wide, 0, 1), ((0, 0), (0, 0), (0, D - D // RING))),
            jnp.pad(jnp.swapaxes(narrow, 0, 1), ((0, 0), (0, 26), (0, D - HD // RING))),
        ],
        axis=1,
    ).astype(jnp.bfloat16)
    last = dict(
        normed=normed, d_qkv=d_qkv, mixed=mixed, d_branch=d_branch, rows=rows.reshape(RING * 32, D)
    )
    kept.update(last)
    if other is None:
        return d_inputs, kept
    picked = {name: chosen(name, last[name]) for name in last}
    grad_attn = (
        inner_rows(picked["normed"], picked["d_qkv"]),
        inner_rows(picked["mixed"], picked["d_branch"]),
        picked["rows"],
    )
    attn_parts = reduce_z_end(reduce_z_begin(place, grad_attn, ATTN_GRAD_PLAN, ATTN_COLS))
    return d_inputs, ffn_parts, attn_parts


GAIN_SIZES = (D, HD, HD, D, D, D)
GAIN_ROWS = (0, 4, 5, 1, 2, 3)


def per_device(
    hidden_in, positions, segments, cotangent,
    query_weight, key_weight, value_weight, output_weight, gate_weight, up_weight, down_weight,
    pre_gain, query_gain, key_gain, mix_gain, ffn_gain, out_gain,
):
    leading = lax.axis_index("section") == 0
    z_index = lax.axis_index("z")
    seq_index = lax.axis_index("y") * RING + lax.axis_index("x")
    place = jnp.reshape(z_index, (1,)).astype(jnp.int32)

    wide = jnp.concatenate([pre_gain, mix_gain, ffn_gain, out_gain])
    narrow = jnp.concatenate([query_gain, key_gain])
    gain_shard = jnp.concatenate(
        [
            jnp.pad(wide, ((0, 0), (0, D - D // RING))),
            jnp.pad(narrow, ((0, 26), (0, D - HD // RING))),
        ]
    )
    attn_arrays = (query_weight[0], key_weight[0], value_weight[0], output_weight[0], gain_shard)
    ffn_arrays = (gate_weight[0], up_weight[0], down_weight[0])
    attn_pieces = gather_weights(pack_shard(attn_arrays, ATTN_PLAN, ATTN_COLS))
    ffn_shard = pack_shard(
        ffn_arrays, FFN_PLAN, FFN_COLS, (attn_pieces[3][0], attn_pieces[4][0])
    )
    ffn_pieces = gather_weights(ffn_shard)
    qkv_w, output_w, corner = unpack_full(
        place, attn_pieces, ATTN_GRAD_PLAN, ATTN_SHAPES, (ffn_shard,)
    )
    attn_w = (qkv_w, output_w)
    corner = corner.reshape(RING, 32, D).astype(jnp.float32)
    gains = [
        corner[:, row, : size // RING].reshape(size) for row, size in zip(GAIN_ROWS, GAIN_SIZES)
    ]
    ffn_w = []

    def await_ffn(mixed):
        mixed = ordered(mixed, ffn_pieces[1][0], ffn_pieces[2][0])
        ffn_w.extend(unpack_full(place, ffn_pieces, FFN_GRAD_PLAN, FFN_SHAPES, (mixed,)))
        return mixed, ffn_w

    exponent = jnp.arange(HD // 2).astype(jnp.float32) * (2.0 / HD)
    freqs = ROPE_BASE ** (-exponent)
    angle = positions[:, 0].reshape(TOKENS).astype(jnp.float32)[:, None] * freqs[None, :]
    tables = (jnp.cos(angle), jnp.sin(angle))

    segment_rows = segments[:, 0]
    anchor = seq_index * SHARD
    padded = jnp.concatenate([jnp.full((MICRO, WINDOW), -1, jnp.int32), segment_rows], axis=1)
    query_seg = lax.dynamic_slice_in_dim(segment_rows, anchor, SHARD, 1)
    key_seg = lax.dynamic_slice_in_dim(padded, anchor, KEYS, 1)
    gap = (jnp.arange(SHARD, dtype=jnp.int32) + WINDOW)[:, None] - jnp.arange(
        KEYS, dtype=jnp.int32
    )[None, :]
    allowed = (gap >= 0) & (gap < WINDOW)
    allowed = allowed[None] & (query_seg[:, :, None] == key_seg[:, None, :])

    first_in = hidden_in[:, 0].reshape(TOKENS, D).astype(jnp.float32)
    first_out, first_kept = forward_layer(
        first_in, tables, allowed, attn_w, gains, 0, await_ffn
    )
    handed = lax.ppermute(first_out, "section", [(0, 1)]).astype(jnp.float32)
    second_out, second_kept = forward_layer(
        handed, tables, allowed, attn_w, gains, 1, lambda mixed: (mixed, ffn_w)
    )

    cot = cotangent[:, 0].reshape(TOKENS, D).astype(jnp.float32)
    d_second, left = backward_layer(cot, second_kept, tables, attn_w, ffn_w, gains, 1)
    d_first_out = lax.ppermute(d_second.astype(jnp.bfloat16), "section", [(1, 0)])
    d_first, ffn_parts, attn_parts = backward_layer(
        d_first_out.astype(jnp.float32), first_kept, tables, attn_w, ffn_w, gains, 0,
        place, leading, left,
    )

    def finish(parts, cols):
        mine = total_of(parts).astype(jnp.bfloat16)
        count = RING * RING
        split = mine.reshape(count, ROWS // count, cols)
        moved = lax.all_to_all(split, ("y", "x"), split_axis=0, concat_axis=0, tiled=True)
        summed = jnp.sum(moved.astype(jnp.float32), axis=0).astype(jnp.bfloat16)
        return lax.all_gather(summed, ("y", "x"), axis=0, tiled=True)

    ffn_done = finish(ffn_parts, FFN_COLS)
    attn_done = finish(attn_parts, ATTN_COLS)

    ffn_outs = unpack_grads(ffn_done, FFN_PLAN, ((160, FF), (160, FF), (512, D)))
    attn_outs = unpack_grads(
        attn_done, ATTN_PLAN, ((160, QH * HD), (160, HD), (160, HD), (256, D), (32, D))
    )
    gain_outs = [
        attn_outs[4][row : row + 1, : size // RING] for row, size in zip(GAIN_ROWS, GAIN_SIZES)
    ]
    outputs = jnp.where(leading, first_out, second_out).reshape(1, MICRO, 1, SHARD, D)
    input_grads = jnp.where(leading, d_first, d_second).reshape(1, MICRO, 1, SHARD, D)
    return (
        outputs,
        input_grads,
        *(item[None] for item in attn_outs[:4]),
        *(item[None] for item in ffn_outs),
        *gain_outs,
    )


def solution(mesh):
    grid = Mesh(
        mesh.devices.reshape(2, RING, RING, RING), ("section", "y", "x", "z")
    )
    seq = ("y", "x")
    in_specs = (
        P(None, "z", seq, None),
        P(None, "z", seq),
        P(None, "z", None),
        P(None, "z", seq, None),
    ) + (P("section", "z", None),) * 7 + (P("section", "z"),) * 6
    out_specs = (
        (P("section", None, "z", seq, None),) * 2
        + (P("section", "z", None),) * 7
        + (P("section", "z"),) * 6
    )
    return jax.shard_map(
        per_device, mesh=grid, in_specs=in_specs, out_specs=out_specs, check_vma=False
    )
```

```python
import jax
import jax.numpy as jnp
import numpy as np
from jax import lax
from jax.experimental import pallas as pl
from jax.experimental.pallas import tpu as pltpu
from jax.sharding import Mesh, PartitionSpec as P

WINDOW = 512
EPSILON = 1e-06
ROPE_BASE = 10000.0

RING = 4
D = 640
FF = 2048
QH = 4
HD = 256
MICRO = 3
SHARD = 128
TOKENS = MICRO * SHARD
HOPS = WINDOW // SHARD
KEYS = SHARD + WINDOW

ROWS = 256
FFN_COLS = 4096
ATTN_COLS = 1920

FFN_PLAN = ((0, 0, 160, 0, 2048, 0, 0), (1, 0, 160, 0, 2048, 0, 2048)) + tuple(
    (2, 96 * i, min(96, 512 - 96 * i), 0, 640, 160, 640 * i) for i in range(6)
)
ATTN_PLAN = (
    (0, 0, 160, 0, 1024, 0, 0),
    (1, 0, 160, 0, 256, 0, 1024),
    (2, 0, 160, 0, 256, 0, 1280),
) + tuple((3, 96 * i, min(96, 256 - 96 * i), 0, 640, 160, 640 * i) for i in range(3)) + (
    (4, 0, 32, 0, 640, 224, 1280),
)

FFN_GRAD_PLAN = ((0, 0, 160, 0, 4096, 0, 0),) + tuple(
    (1, 96 * i, min(96, 512 - 96 * i), 0, 640, 160, 640 * i) for i in range(6)
)
ATTN_GRAD_PLAN = (
    ((0, 0, 160, 0, 1536, 0, 0),)
    + tuple((1, 96 * i, min(96, 256 - 96 * i), 0, 640, 160, 640 * i) for i in range(3))
    + ((2, 0, 32, 0, 640, 224, 1280),)
)


def in_any(count):
    return [pl.BlockSpec(memory_space=pl.ANY)] * count


def in_vmem(count):
    return [pl.BlockSpec(memory_space=pltpu.VMEM)] * count


LIMIT = 24 * 1024 * 1024


def run_copies(copies):
    for item in copies:
        item.start()
    for item in copies:
        item.wait()


def pack_shard(arrays, plan, cols, after=()):
    def body(*refs):
        sources, out, sems = refs[: len(arrays)], refs[-2], refs[-1]
        run_copies(
            [
                pltpu.make_async_copy(
                    sources[a].at[pl.ds(r, n), pl.ds(c, w)],
                    out.at[pl.ds(pr, n), pl.ds(pc, w)],
                    sems.at[i],
                )
                for i, (a, r, n, c, w, pr, pc) in enumerate(plan)
            ]
        )

    return pl.pallas_call(
        body,
        in_specs=in_any(len(arrays) + len(after)),
        out_specs=pl.BlockSpec(memory_space=pltpu.VMEM),
        out_shape=jax.ShapeDtypeStruct((ROWS, cols), jnp.bfloat16),
        compiler_params=pltpu.CompilerParams(vmem_limit_bytes=LIMIT),
        scratch_shapes=[pltpu.SemaphoreType.DMA((len(plan),))],
        name="pack_shard",
    )(*arrays, *after)


def ordered(value, *after):
    return pl.pallas_call(
        lambda *refs: None,
        in_specs=in_any(1 + len(after)),
        out_specs=pl.BlockSpec(memory_space=pl.ANY),
        out_shape=jax.ShapeDtypeStruct(value.shape, value.dtype),
        input_output_aliases={0: 0},
        name="ordered",
    )(value, *after)


def unpack_full(place, pieces, plan, shapes, after=()):
    arrays = [item[0] for item in pieces]
    jobs = []
    for index, (_, rel, first, count) in enumerate(pieces):
        for a, r, n, c, w, pr, pc in plan:
            low, high = max(pr, first), min(pr + n, first + count)
            if low < high:
                jobs.append((index, rel, low - first, pc, a, r + low - pr, c, high - low, w))

    def body(place_ref, *refs):
        sources = refs[: len(arrays)]
        outs = refs[-1 - len(shapes) : -1]
        sems = refs[-1]
        here = place_ref[0]
        copies = []
        for i, (index, rel, sr, sc, a, r, c, n, w) in enumerate(jobs):
            block = lax.rem(here + rel, RING)
            rows = shapes[a][0] // RING
            start = pl.multiple_of(block * rows + r, 32)
            copies.append(
                pltpu.make_async_copy(
                    sources[index].at[pl.ds(sr, n), pl.ds(sc, w)],
                    outs[a].at[pl.ds(start, n), pl.ds(c, w)],
                    sems.at[i],
                )
            )
        run_copies(copies)

    return pl.pallas_call(
        body,
        in_specs=[pl.BlockSpec(memory_space=pltpu.SMEM)] + in_any(len(arrays) + len(after)),
        out_specs=in_vmem(len(shapes)),
        compiler_params=pltpu.CompilerParams(vmem_limit_bytes=LIMIT),
        out_shape=[jax.ShapeDtypeStruct(shape, jnp.bfloat16) for shape in shapes],
        scratch_shapes=[pltpu.SemaphoreType.DMA((len(jobs),))],
        name="unpack_full",
    )(place, *arrays, *after)


def pack_blocks(place, arrays, plan, cols, after=()):
    half = ROWS // 2
    targets = [(0, 0, ROWS), (1, 0, ROWS), (3, 0, ROWS), (2, 0, half), (2, half, half)]
    jobs = []
    for index, (rel, first, count) in enumerate(targets):
        for a, r, n, c, w, pr, pc in plan:
            low, high = max(pr, first), min(pr + n, first + count)
            if low < high:
                jobs.append((index, rel, low - first, pc, a, r + low - pr, c, high - low, w))

    def body(place_ref, *refs):
        sources = refs[: len(arrays)]
        outs = refs[-1 - len(targets) : -1]
        sems = refs[-1]
        here = place_ref[0]
        copies = []
        for i, (index, rel, sr, sc, a, r, c, n, w) in enumerate(jobs):
            block = lax.rem(here + rel, RING)
            rows = arrays[a].shape[0] // RING
            start = pl.multiple_of(block * rows + r, 32)
            copies.append(
                pltpu.make_async_copy(
                    sources[a].at[pl.ds(start, n), pl.ds(c, w)],
                    outs[index].at[pl.ds(sr, n), pl.ds(sc, w)],
                    sems.at[i],
                )
            )
        run_copies(copies)

    return pl.pallas_call(
        body,
        in_specs=[pl.BlockSpec(memory_space=pltpu.SMEM)] + in_any(len(arrays) + len(after)),
        out_specs=in_vmem(len(targets)),
        compiler_params=pltpu.CompilerParams(vmem_limit_bytes=LIMIT),
        out_shape=[jax.ShapeDtypeStruct((t[2], cols), jnp.bfloat16) for t in targets],
        scratch_shapes=[pltpu.SemaphoreType.DMA((len(jobs),))],
        name="pack_blocks",
    )(place, *arrays, *after)


def along_z(x, by):
    return lax.ppermute(x, "z", [(i, (i + by) % RING) for i in range(RING)])


def along_seq(x, section, by):
    count = RING * RING
    pairs = [
        (section * count + i, section * count + i + by) for i in range(count) if 0 <= i + by < count
    ]
    return lax.ppermute(x, ("section", "y", "x"), pairs)


def gather_weights(shard):
    half = ROWS // 2
    above = along_z(shard, -1)
    below = along_z(shard, 1)
    passed = (below[:half], above[half:])
    first = along_z(passed[0], 1)
    second = along_z(passed[1], -1)
    pieces = (
        (shard, 0, 0, ROWS),
        (above, 1, 0, ROWS),
        (below, 3, 0, ROWS),
        (first, 2, 0, half),
        (second, 2, half, half),
    )
    return pieces, passed


def reduce_z_begin(place, arrays, plan, cols, after=()):
    own, next_up, next_down, far_a, far_b = pack_blocks(place, arrays, plan, cols, after)
    return own, next_up, next_down, along_z(far_a, 1), along_z(far_b, -1)


def reduce_z_end(begun):
    own, after, before, got_a, got_b = begun
    half = ROWS // 2
    after = lax.dynamic_update_slice(after, after[:half] + got_a, (0, 0))
    before = lax.dynamic_update_slice(before, before[half:] + got_b, (half, 0))
    return own, along_z(after, 1), along_z(before, -1)


def unpack_grads(packed, plan, shapes):
    def body(source, *outs):
        for a, r, n, c, w, pr, pc in plan:
            outs[a][pl.ds(r, n), pl.ds(c, w)] = source[pl.ds(pr, n), pl.ds(pc, w)].astype(
                jnp.float32
            )

    return pl.pallas_call(
        body,
        in_specs=in_vmem(1),
        out_specs=in_vmem(len(shapes)),
        out_shape=[jax.ShapeDtypeStruct(shape, jnp.float32) for shape in shapes],
        compiler_params=pltpu.CompilerParams(vmem_limit_bytes=LIMIT),
        name="unpack_grads",
    )(packed)


def total_of(parts):
    own, left, right = (item.astype(jnp.float32) for item in parts)
    return own + left + right


def normalize(values, gain):
    return values * lax.rsqrt(jnp.mean(values * values, axis=-1, keepdims=True) + EPSILON) * gain


def product(left, right):
    return jnp.dot(left, right, preferred_element_type=jnp.float32)


def inner_rows(left, right):
    return lax.dot_general(
        left, right, (((0,), (0,)), ((), ())), preferred_element_type=jnp.float32
    ).astype(jnp.bfloat16)


def against(left, right):
    return lax.dot_general(
        left, right, (((1,), (1,)), ((), ())), preferred_element_type=jnp.float32
    )


def turn(values, cosine, sine):
    half = values.shape[-1] // 2
    former = values[..., :half]
    latter = values[..., half:]
    return jnp.concatenate(
        [former * cosine - latter * sine, latter * cosine + former * sine], axis=-1
    )


def batched(spec, left, right):
    return jnp.einsum(spec, left, right, preferred_element_type=jnp.float32)


def forward_layer(inputs, tables, allowed, attn_w, gains, section, ffn_weights):
    qkv_w, output_w = attn_w
    pre_g, query_g, key_g, mix_g, ffn_g, out_g = gains
    cosine, sine = tables
    normed = normalize(inputs, pre_g).astype(jnp.bfloat16)
    key_value = product(normed, qkv_w[:, QH * HD :])
    key_raw = key_value[:, :HD]
    values = key_value[:, HD:].astype(jnp.bfloat16)
    key_rot = turn(normalize(key_raw, key_g), cosine, sine).astype(jnp.bfloat16)
    own = jnp.stack([key_rot, values]).reshape(2, MICRO, SHARD, HD)
    pieces = [along_seq(own, section, by) for by in range(HOPS, 0, -1)]
    query_raw = product(normed, qkv_w[:, : QH * HD]).reshape(MICRO, SHARD, QH, HD)
    query_raw = jnp.swapaxes(query_raw, 1, 2)
    query_rot = turn(
        normalize(query_raw, query_g),
        cosine.reshape(MICRO, 1, SHARD, HD // 2),
        sine.reshape(MICRO, 1, SHARD, HD // 2),
    ).astype(jnp.bfloat16)
    joined = jnp.concatenate(pieces + [own], axis=2)
    keys_all, values_all = joined[0], joined[1]
    raw = batched("mhqd,mkd->mhqk", query_rot, keys_all)
    score = jnp.where(allowed[:, None], raw * HD ** (-0.5), -1e30)
    highest = jnp.max(score, axis=-1, keepdims=True)
    expo = jnp.exp(score - highest)
    prob = expo / jnp.sum(expo, axis=-1, keepdims=True)
    mixed = batched("mhqk,mkd->mhqd", prob.astype(jnp.bfloat16), values_all).astype(jnp.bfloat16)
    mixed = jnp.swapaxes(mixed, 1, 2).reshape(TOKENS, QH * HD)
    mixed, (gate_up_w, down_w) = ffn_weights(mixed)
    branch = product(mixed, output_w)
    middle = inputs + normalize(branch, mix_g)
    inner = normalize(middle, ffn_g).astype(jnp.bfloat16)
    gate_up = product(inner, gate_up_w)
    gate_act = gate_up[:, :FF]
    up_act = gate_up[:, FF:]
    hidden = (jax.nn.gelu(gate_act) * up_act).astype(jnp.bfloat16)
    down = product(hidden, down_w)
    result = (middle + normalize(down, out_g)).astype(jnp.bfloat16)
    stored = (
        inputs, normed, query_raw, key_raw, query_rot, keys_all, values_all, prob, mixed, branch,
        middle, inner, gate_act, up_act, hidden, down,
    )
    return result, stored


ATTN_SHAPES = ((D, QH * HD + 2 * HD), (QH * HD, D), (RING * 32, D))
FFN_SHAPES = ((D, 2 * FF), (FF, D))


def norm_back(grad, values, gain):
    scale = lax.rsqrt(jnp.mean(values * values, axis=-1, keepdims=True) + EPSILON)
    unit = values * scale
    weighted = grad * gain
    dv = scale * (weighted - unit * jnp.mean(weighted * unit, axis=-1, keepdims=True))
    return dv, grad * unit


def backward_layer(
    grad_out, stored, tables, attn_w, ffn_w, gains, section, place=None, leading=None, other=None
):
    def chosen(name, mine):
        return jnp.where(leading, mine, other[name])

    kept = {}
    (
        inputs, normed, query_raw, key_raw, query_rot, keys_all, values_all, prob, mixed, branch,
        middle, inner, gate_act, up_act, hidden, down,
    ) = stored
    qkv_w, output_w = attn_w
    gate_up_w, down_w = ffn_w
    pre_g, query_g, key_g, mix_g, ffn_g, out_g = gains
    cosine, sine = tables
    d_down, by_out = norm_back(grad_out, down, out_g)
    d_out_g = jnp.sum(by_out, axis=0)
    d_down = d_down.astype(jnp.bfloat16)
    d_hidden = against(d_down, down_w)
    _, pull = jax.vjp(
        lambda gate_in, up_in: jax.nn.gelu(gate_in) * up_in, gate_act, up_act
    )
    d_gate, d_up = pull(d_hidden)
    d_gate_up = jnp.concatenate([d_gate.astype(jnp.bfloat16), d_up.astype(jnp.bfloat16)], axis=1)
    kept.update(inner=inner, d_gate_up=d_gate_up, hidden=hidden, d_down=d_down)
    if other is not None:
        picked = {name: chosen(name, kept[name]) for name in kept}
        grad_ffn = (
            inner_rows(picked["inner"], picked["d_gate_up"]),
            inner_rows(picked["hidden"], picked["d_down"]),
        )
        ffn_begun = reduce_z_begin(place, grad_ffn, FFN_GRAD_PLAN, FFN_COLS)
    d_inner = against(d_gate_up, gate_up_w)
    d_middle_ffn, by_ffn = norm_back(d_inner, middle, ffn_g)
    d_ffn_g = jnp.sum(by_ffn, axis=0)
    d_middle = grad_out + d_middle_ffn
    d_branch, by_mix = norm_back(d_middle, branch, mix_g)
    d_mix_g = jnp.sum(by_mix, axis=0)
    d_branch = d_branch.astype(jnp.bfloat16)
    d_mixed = against(d_branch, output_w).astype(jnp.bfloat16)
    if other is not None:
        d_mixed = ordered(d_mixed, ffn_begun[0])
    d_mixed = jnp.swapaxes(d_mixed.reshape(MICRO, SHARD, QH, HD), 1, 2)
    d_prob = batched("mhqd,mkd->mhqk", d_mixed, values_all)
    d_score = (prob * (d_prob - jnp.sum(prob * d_prob, axis=-1, keepdims=True))).astype(
        jnp.bfloat16
    )
    scale = HD ** (-0.5)
    d_keys = batched("mhqk,mhqd->mkd", d_score, query_rot) * scale
    if other is not None:
        d_keys = ordered(d_keys, ffn_begun[3], ffn_begun[4])
        ffn_parts = reduce_z_end(ffn_begun)
    d_values_all = batched("mhqk,mhqd->mkd", prob.astype(jnp.bfloat16), d_mixed)
    d_stacked = jnp.stack([d_keys, d_values_all])
    back = d_stacked[:, :, HOPS * SHARD :]
    for offset in range(HOPS):
        piece = d_stacked[:, :, offset * SHARD : (offset + 1) * SHARD].astype(jnp.bfloat16)
        back = back + along_seq(piece, section, offset - HOPS).astype(jnp.float32)
    back = back.reshape(2, TOKENS, HD)
    d_query_rot = batched("mhqk,mkd->mhqd", d_score, keys_all) * scale
    d_query, by_query = norm_back(
        turn(
            d_query_rot,
            cosine.reshape(MICRO, 1, SHARD, HD // 2),
            -sine.reshape(MICRO, 1, SHARD, HD // 2),
        ),
        query_raw,
        query_g,
    )
    d_query_g = jnp.sum(by_query, axis=(0, 1, 2))
    d_query = jnp.swapaxes(d_query.astype(jnp.bfloat16), 1, 2).reshape(TOKENS, QH * HD)
    d_values = back[1].astype(jnp.bfloat16)
    d_key, by_key = norm_back(turn(back[0], cosine, -sine), key_raw, key_g)
    d_key_g = jnp.sum(by_key, axis=0)
    d_qkv = jnp.concatenate([d_query, d_key.astype(jnp.bfloat16), d_values], axis=1)
    d_normed = against(d_qkv, qkv_w)
    d_inputs_pre, by_pre = norm_back(d_normed, inputs, pre_g)
    d_pre_g = jnp.sum(by_pre, axis=0)
    d_inputs = d_middle + d_inputs_pre
    wide = jnp.stack([d_pre_g, d_mix_g, d_ffn_g, d_out_g]).reshape(4, RING, D // RING)
    narrow = jnp.stack([d_query_g, d_key_g]).reshape(2, RING, HD // RING)
    rows = jnp.concatenate(
        [
            jnp.pad(jnp.swapaxes(wide, 0, 1), ((0, 0), (0, 0), (0, D - D // RING))),
            jnp.pad(jnp.swapaxes(narrow, 0, 1), ((0, 0), (0, 26), (0, D - HD // RING))),
        ],
        axis=1,
    ).astype(jnp.bfloat16)
    last = dict(
        normed=normed, d_qkv=d_qkv, mixed=mixed, d_branch=d_branch, rows=rows.reshape(RING * 32, D)
    )
    kept.update(last)
    if other is None:
        return d_inputs, kept
    picked = {name: chosen(name, last[name]) for name in last}
    grad_attn = (
        inner_rows(picked["normed"], picked["d_qkv"]),
        inner_rows(picked["mixed"], picked["d_branch"]),
        picked["rows"],
    )
    attn_parts = reduce_z_end(
        reduce_z_begin(place, grad_attn, ATTN_GRAD_PLAN, ATTN_COLS, ffn_parts[1:])
    )
    return d_inputs, ffn_parts, attn_parts


GAIN_SIZES = (D, HD, HD, D, D, D)
GAIN_ROWS = (0, 4, 5, 1, 2, 3)


def per_device(
    hidden_in, positions, segments, cotangent,
    query_weight, key_weight, value_weight, output_weight, gate_weight, up_weight, down_weight,
    pre_gain, query_gain, key_gain, mix_gain, ffn_gain, out_gain,
):
    leading = lax.axis_index("section") == 0
    z_index = lax.axis_index("z")
    seq_index = lax.axis_index("y") * RING + lax.axis_index("x")
    place = jnp.reshape(z_index, (1,)).astype(jnp.int32)

    wide = jnp.concatenate([pre_gain, mix_gain, ffn_gain, out_gain])
    narrow = jnp.concatenate([query_gain, key_gain])
    gain_shard = jnp.concatenate(
        [
            jnp.pad(wide, ((0, 0), (0, D - D // RING))),
            jnp.pad(narrow, ((0, 26), (0, D - HD // RING))),
        ]
    )
    attn_arrays = (query_weight[0], key_weight[0], value_weight[0], output_weight[0], gain_shard)
    ffn_arrays = (gate_weight[0], up_weight[0], down_weight[0])
    attn_pieces, passed = gather_weights(pack_shard(attn_arrays, ATTN_PLAN, ATTN_COLS))
    ffn_shard = pack_shard(ffn_arrays, FFN_PLAN, FFN_COLS, passed)
    ffn_pieces, _ = gather_weights(ffn_shard)
    qkv_w, output_w, corner = unpack_full(
        place, attn_pieces, ATTN_GRAD_PLAN, ATTN_SHAPES, (ffn_shard,)
    )
    attn_w = (qkv_w, output_w)
    corner = corner.reshape(RING, 32, D).astype(jnp.float32)
    gains = [
        corner[:, row, : size // RING].reshape(size) for row, size in zip(GAIN_ROWS, GAIN_SIZES)
    ]
    ffn_w = []

    def await_ffn(mixed):
        mixed = ordered(mixed, ffn_pieces[1][0], ffn_pieces[2][0])
        ffn_w.extend(unpack_full(place, ffn_pieces, FFN_GRAD_PLAN, FFN_SHAPES, (mixed,)))
        return mixed, ffn_w

    exponent = jnp.arange(HD // 2).astype(jnp.float32) * (2.0 / HD)
    freqs = ROPE_BASE ** (-exponent)
    angle = positions[:, 0].reshape(TOKENS).astype(jnp.float32)[:, None] * freqs[None, :]
    tables = (jnp.cos(angle), jnp.sin(angle))

    segment_rows = segments[:, 0]
    anchor = seq_index * SHARD
    padded = jnp.concatenate([jnp.full((MICRO, WINDOW), -1, jnp.int32), segment_rows], axis=1)
    query_seg = lax.dynamic_slice_in_dim(segment_rows, anchor, SHARD, 1)
    key_seg = lax.dynamic_slice_in_dim(padded, anchor, KEYS, 1)
    gap = (jnp.arange(SHARD, dtype=jnp.int32) + WINDOW)[:, None] - jnp.arange(
        KEYS, dtype=jnp.int32
    )[None, :]
    allowed = (gap >= 0) & (gap < WINDOW)
    allowed = allowed[None] & (query_seg[:, :, None] == key_seg[:, None, :])

    first_in = hidden_in[:, 0].reshape(TOKENS, D).astype(jnp.float32)
    first_out, first_kept = forward_layer(
        first_in, tables, allowed, attn_w, gains, 0, await_ffn
    )
    handed = lax.ppermute(first_out, "section", [(0, 1)]).astype(jnp.float32)
    second_out, second_kept = forward_layer(
        handed, tables, allowed, attn_w, gains, 1, lambda mixed: (mixed, ffn_w)
    )

    cot = cotangent[:, 0].reshape(TOKENS, D).astype(jnp.float32)
    d_second, left = backward_layer(cot, second_kept, tables, attn_w, ffn_w, gains, 1)
    d_first_out = lax.ppermute(d_second.astype(jnp.bfloat16), "section", [(1, 0)])
    d_first, ffn_parts, attn_parts = backward_layer(
        d_first_out.astype(jnp.float32), first_kept, tables, attn_w, ffn_w, gains, 0,
        place, leading, left,
    )

    def finish(parts, cols):
        mine = total_of(parts).astype(jnp.bfloat16)
        count = RING * RING
        split = mine.reshape(count, ROWS // count, cols)
        moved = lax.all_to_all(split, ("y", "x"), split_axis=0, concat_axis=0, tiled=True)
        summed = jnp.sum(moved.astype(jnp.float32), axis=0).astype(jnp.bfloat16)
        return lax.all_gather(summed, ("y", "x"), axis=0, tiled=True)

    ffn_done = finish(ffn_parts, FFN_COLS)
    attn_done = finish(attn_parts, ATTN_COLS)

    ffn_outs = unpack_grads(ffn_done, FFN_PLAN, ((160, FF), (160, FF), (512, D)))
    attn_outs = unpack_grads(
        attn_done, ATTN_PLAN, ((160, QH * HD), (160, HD), (160, HD), (256, D), (32, D))
    )
    gain_outs = [
        attn_outs[4][row : row + 1, : size // RING] for row, size in zip(GAIN_ROWS, GAIN_SIZES)
    ]
    outputs = jnp.where(leading, first_out, second_out).reshape(1, MICRO, 1, SHARD, D)
    input_grads = jnp.where(leading, d_first, d_second).reshape(1, MICRO, 1, SHARD, D)
    return (
        outputs,
        input_grads,
        *(item[None] for item in attn_outs[:4]),
        *(item[None] for item in ffn_outs),
        *gain_outs,
    )


def solution(mesh):
    grid = Mesh(
        mesh.devices.reshape(2, RING, RING, RING), ("section", "y", "x", "z")
    )
    seq = ("y", "x")
    in_specs = (
        P(None, "z", seq, None),
        P(None, "z", seq),
        P(None, "z", None),
        P(None, "z", seq, None),
    ) + (P("section", "z", None),) * 7 + (P("section", "z"),) * 6
    out_specs = (
        (P("section", None, "z", seq, None),) * 2
        + (P("section", "z", None),) * 7
        + (P("section", "z"),) * 6
    )
    return jax.shard_map(
        per_device, mesh=grid, in_specs=in_specs, out_specs=out_specs, check_vma=False
    )
```

```python
import jax
import jax.numpy as jnp
import numpy as np
from jax import lax
from jax.experimental import pallas as pl
from jax.experimental.pallas import tpu as pltpu
from jax.sharding import Mesh, PartitionSpec as P

WINDOW = 512
EPSILON = 1e-06
ROPE_BASE = 10000.0

RING = 4
D = 640
FF = 2048
QH = 4
HD = 256
MICRO = 3
SHARD = 128
TOKENS = MICRO * SHARD
HOPS = WINDOW // SHARD
KEYS = SHARD + WINDOW

ROWS = 256
FFN_COLS = 4096
ATTN_COLS = 1920

FFN_PLAN = ((0, 0, 160, 0, 2048, 0, 0), (1, 0, 160, 0, 2048, 0, 2048)) + tuple(
    (2, 96 * i, min(96, 512 - 96 * i), 0, 640, 160, 640 * i) for i in range(6)
)
ATTN_PLAN = (
    (0, 0, 160, 0, 1024, 0, 0),
    (1, 0, 160, 0, 256, 0, 1024),
    (2, 0, 160, 0, 256, 0, 1280),
) + tuple((3, 96 * i, min(96, 256 - 96 * i), 0, 640, 160, 640 * i) for i in range(3)) + (
    (4, 0, 32, 0, 640, 224, 1280),
)

FFN_GRAD_PLAN = ((0, 0, 160, 0, 4096, 0, 0),) + tuple(
    (1, 96 * i, min(96, 512 - 96 * i), 0, 640, 160, 640 * i) for i in range(6)
)
ATTN_GRAD_PLAN = (
    ((0, 0, 160, 0, 1536, 0, 0),)
    + tuple((1, 96 * i, min(96, 256 - 96 * i), 0, 640, 160, 640 * i) for i in range(3))
    + ((2, 0, 32, 0, 640, 224, 1280),)
)


EARLY_COLS = 5120
LATE_COLS = 1024
EARLY_PLAN = FFN_GRAD_PLAN + (
    (2, 0, 64, 0, 640, 192, 3200),
    (2, 64, 96, 0, 640, 160, 3840),
    (2, 160, 96, 0, 640, 160, 4480),
)
LATE_PLAN = (
    (0, 0, 160, 0, 1024, 0, 0),
    (0, 0, 96, 1024, 512, 160, 0),
    (0, 96, 64, 1024, 512, 160, 512),
    (1, 0, 32, 0, 512, 224, 512),
)
EARLY_OUT = FFN_PLAN + tuple((3,) + item[1:] for item in EARLY_PLAN[-3:])
LATE_OUT = (
    (0, 0, 160, 0, 1024, 0, 0),
    (1, 0, 96, 0, 256, 160, 0),
    (1, 96, 64, 0, 256, 160, 512),
    (2, 0, 96, 0, 256, 160, 256),
    (2, 96, 64, 0, 256, 160, 768),
    (3, 0, 32, 0, 512, 224, 512),
)


def in_any(count):
    return [pl.BlockSpec(memory_space=pl.ANY)] * count


def in_vmem(count):
    return [pl.BlockSpec(memory_space=pltpu.VMEM)] * count


LIMIT = 24 * 1024 * 1024


def run_copies(copies):
    for item in copies:
        item.start()
    for item in copies:
        item.wait()


def pack_shard(arrays, plan, cols, after=()):
    def body(*refs):
        sources, out, sems = refs[: len(arrays)], refs[-2], refs[-1]
        run_copies(
            [
                pltpu.make_async_copy(
                    sources[a].at[pl.ds(r, n), pl.ds(c, w)],
                    out.at[pl.ds(pr, n), pl.ds(pc, w)],
                    sems.at[i],
                )
                for i, (a, r, n, c, w, pr, pc) in enumerate(plan)
            ]
        )

    return pl.pallas_call(
        body,
        in_specs=in_any(len(arrays) + len(after)),
        out_specs=pl.BlockSpec(memory_space=pltpu.VMEM),
        out_shape=jax.ShapeDtypeStruct((ROWS, cols), jnp.bfloat16),
        compiler_params=pltpu.CompilerParams(vmem_limit_bytes=LIMIT),
        scratch_shapes=[pltpu.SemaphoreType.DMA((len(plan),))],
        name="pack_shard",
    )(*arrays, *after)


def ordered(value, *after):
    return pl.pallas_call(
        lambda *refs: None,
        in_specs=in_any(1 + len(after)),
        out_specs=pl.BlockSpec(memory_space=pl.ANY),
        out_shape=jax.ShapeDtypeStruct(value.shape, value.dtype),
        input_output_aliases={0: 0},
        name="ordered",
    )(value, *after)


def unpack_full(place, pieces, plan, shapes, after=()):
    arrays = [item[0] for item in pieces]
    jobs = []
    for index, (_, rel, first, count) in enumerate(pieces):
        for a, r, n, c, w, pr, pc in plan:
            low, high = max(pr, first), min(pr + n, first + count)
            if low < high:
                jobs.append((index, rel, low - first, pc, a, r + low - pr, c, high - low, w))

    def body(place_ref, *refs):
        sources = refs[: len(arrays)]
        outs = refs[-1 - len(shapes) : -1]
        sems = refs[-1]
        here = place_ref[0]
        copies = []
        for i, (index, rel, sr, sc, a, r, c, n, w) in enumerate(jobs):
            block = lax.rem(here + rel, RING)
            rows = shapes[a][0] // RING
            start = pl.multiple_of(block * rows + r, 32)
            copies.append(
                pltpu.make_async_copy(
                    sources[index].at[pl.ds(sr, n), pl.ds(sc, w)],
                    outs[a].at[pl.ds(start, n), pl.ds(c, w)],
                    sems.at[i],
                )
            )
        run_copies(copies)

    return pl.pallas_call(
        body,
        in_specs=[pl.BlockSpec(memory_space=pltpu.SMEM)] + in_any(len(arrays) + len(after)),
        out_specs=in_vmem(len(shapes)),
        compiler_params=pltpu.CompilerParams(vmem_limit_bytes=LIMIT),
        out_shape=[jax.ShapeDtypeStruct(shape, jnp.bfloat16) for shape in shapes],
        scratch_shapes=[pltpu.SemaphoreType.DMA((len(jobs),))],
        name="unpack_full",
    )(place, *arrays, *after)


def pack_blocks(place, arrays, plan, cols, after=()):
    half = ROWS // 2
    targets = [(0, 0, ROWS), (1, 0, ROWS), (3, 0, ROWS), (2, 0, half), (2, half, half)]
    jobs = []
    for index, (rel, first, count) in enumerate(targets):
        for a, r, n, c, w, pr, pc in plan:
            low, high = max(pr, first), min(pr + n, first + count)
            if low < high:
                jobs.append((index, rel, low - first, pc, a, r + low - pr, c, high - low, w))

    def body(place_ref, *refs):
        sources = refs[: len(arrays)]
        outs = refs[-1 - len(targets) : -1]
        sems = refs[-1]
        here = place_ref[0]
        copies = []
        for i, (index, rel, sr, sc, a, r, c, n, w) in enumerate(jobs):
            block = lax.rem(here + rel, RING)
            rows = arrays[a].shape[0] // RING
            start = pl.multiple_of(block * rows + r, 32)
            copies.append(
                pltpu.make_async_copy(
                    sources[a].at[pl.ds(start, n), pl.ds(c, w)],
                    outs[index].at[pl.ds(sr, n), pl.ds(sc, w)],
                    sems.at[i],
                )
            )
        run_copies(copies)

    return pl.pallas_call(
        body,
        in_specs=[pl.BlockSpec(memory_space=pltpu.SMEM)] + in_any(len(arrays) + len(after)),
        out_specs=in_vmem(len(targets)),
        compiler_params=pltpu.CompilerParams(vmem_limit_bytes=LIMIT),
        out_shape=[jax.ShapeDtypeStruct((t[2], cols), jnp.bfloat16) for t in targets],
        scratch_shapes=[pltpu.SemaphoreType.DMA((len(jobs),))],
        name="pack_blocks",
    )(place, *arrays, *after)


def along_z(x, by):
    return lax.ppermute(x, "z", [(i, (i + by) % RING) for i in range(RING)])


def along_seq(x, section, by):
    count = RING * RING
    pairs = [
        (section * count + i, section * count + i + by) for i in range(count) if 0 <= i + by < count
    ]
    return lax.ppermute(x, ("section", "y", "x"), pairs)


def gather_weights(shard):
    half = ROWS // 2
    above = along_z(shard, -1)
    below = along_z(shard, 1)
    passed = (below[:half], above[half:])
    first = along_z(passed[0], 1)
    second = along_z(passed[1], -1)
    pieces = (
        (shard, 0, 0, ROWS),
        (above, 1, 0, ROWS),
        (below, 3, 0, ROWS),
        (first, 2, 0, half),
        (second, 2, half, half),
    )
    return pieces, passed


def reduce_z_begin(place, arrays, plan, cols, after=()):
    own, next_up, next_down, far_a, far_b = pack_blocks(place, arrays, plan, cols, after)
    return own, next_up, next_down, along_z(far_a, 1), along_z(far_b, -1)


def reduce_z_end(begun):
    own, after, before, got_a, got_b = begun
    half = ROWS // 2
    after = lax.dynamic_update_slice(after, after[:half] + got_a, (0, 0))
    before = lax.dynamic_update_slice(before, before[half:] + got_b, (half, 0))
    return own, along_z(after, 1), along_z(before, -1)


def unpack_grads(packed, plan, shapes):
    def body(source, *outs):
        for a, r, n, c, w, pr, pc in plan:
            outs[a][pl.ds(r, n), pl.ds(c, w)] = source[pl.ds(pr, n), pl.ds(pc, w)].astype(
                jnp.float32
            )

    return pl.pallas_call(
        body,
        in_specs=in_vmem(1),
        out_specs=in_vmem(len(shapes)),
        out_shape=[jax.ShapeDtypeStruct(shape, jnp.float32) for shape in shapes],
        compiler_params=pltpu.CompilerParams(vmem_limit_bytes=LIMIT),
        name="unpack_grads",
    )(packed)


def total_of(parts):
    own, left, right = (item.astype(jnp.float32) for item in parts)
    return own + left + right


def normalize(values, gain):
    return values * lax.rsqrt(jnp.mean(values * values, axis=-1, keepdims=True) + EPSILON) * gain


def product(left, right):
    return jnp.dot(left, right, preferred_element_type=jnp.float32)


def inner_rows(left, right):
    return lax.dot_general(
        left, right, (((0,), (0,)), ((), ())), preferred_element_type=jnp.float32
    ).astype(jnp.bfloat16)


def against(left, right):
    return lax.dot_general(
        left, right, (((1,), (1,)), ((), ())), preferred_element_type=jnp.float32
    )


def turn(values, cosine, sine):
    half = values.shape[-1] // 2
    former = values[..., :half]
    latter = values[..., half:]
    return jnp.concatenate(
        [former * cosine - latter * sine, latter * cosine + former * sine], axis=-1
    )


def batched(spec, left, right):
    return jnp.einsum(spec, left, right, preferred_element_type=jnp.float32)


def forward_layer(inputs, tables, allowed, attn_w, gains, section, ffn_weights):
    qkv_w, output_w = attn_w
    pre_g, query_g, key_g, mix_g, ffn_g, out_g = gains
    cosine, sine = tables
    normed = normalize(inputs, pre_g).astype(jnp.bfloat16)
    key_value = product(normed, qkv_w[:, QH * HD :])
    key_raw = key_value[:, :HD]
    values = key_value[:, HD:].astype(jnp.bfloat16)
    key_rot = turn(normalize(key_raw, key_g), cosine, sine).astype(jnp.bfloat16)
    own = jnp.stack([key_rot, values]).reshape(2, MICRO, SHARD, HD)
    pieces = [along_seq(own, section, by) for by in range(HOPS, 0, -1)]
    query_raw = product(normed, qkv_w[:, : QH * HD]).reshape(MICRO, SHARD, QH, HD)
    query_raw = jnp.swapaxes(query_raw, 1, 2)
    query_rot = turn(
        normalize(query_raw, query_g),
        cosine.reshape(MICRO, 1, SHARD, HD // 2),
        sine.reshape(MICRO, 1, SHARD, HD // 2),
    ).astype(jnp.bfloat16)
    joined = jnp.concatenate(pieces + [own], axis=2)
    keys_all, values_all = joined[0], joined[1]
    raw = batched("mhqd,mkd->mhqk", query_rot, keys_all)
    score = jnp.where(allowed[:, None], raw * HD ** (-0.5), -1e30)
    highest = jnp.max(score, axis=-1, keepdims=True)
    expo = jnp.exp(score - highest)
    prob = expo / jnp.sum(expo, axis=-1, keepdims=True)
    mixed = batched("mhqk,mkd->mhqd", prob.astype(jnp.bfloat16), values_all).astype(jnp.bfloat16)
    mixed = jnp.swapaxes(mixed, 1, 2).reshape(TOKENS, QH * HD)
    mixed, (gate_up_w, down_w) = ffn_weights(mixed)
    branch = product(mixed, output_w)
    middle = inputs + normalize(branch, mix_g)
    inner = normalize(middle, ffn_g).astype(jnp.bfloat16)
    gate_up = product(inner, gate_up_w)
    gate_act = gate_up[:, :FF]
    up_act = gate_up[:, FF:]
    hidden = (jax.nn.gelu(gate_act) * up_act).astype(jnp.bfloat16)
    down = product(hidden, down_w)
    result = (middle + normalize(down, out_g)).astype(jnp.bfloat16)
    stored = (
        inputs, normed, query_raw, key_raw, query_rot, keys_all, values_all, prob, mixed, branch,
        middle, inner, gate_act, up_act, hidden, down,
    )
    return result, stored


ATTN_SHAPES = ((D, QH * HD + 2 * HD), (QH * HD, D), (RING * 32, D))
FFN_SHAPES = ((D, 2 * FF), (FF, D))


def norm_back(grad, values, gain):
    scale = lax.rsqrt(jnp.mean(values * values, axis=-1, keepdims=True) + EPSILON)
    unit = values * scale
    weighted = grad * gain
    dv = scale * (weighted - unit * jnp.mean(weighted * unit, axis=-1, keepdims=True))
    return dv, grad * unit


def backward_layer(
    grad_out, stored, tables, attn_w, ffn_w, gains, section, place=None, leading=None, other=None
):
    def chosen(name, mine):
        return jnp.where(leading, mine, other[name])

    kept = {}
    (
        inputs, normed, query_raw, key_raw, query_rot, keys_all, values_all, prob, mixed, branch,
        middle, inner, gate_act, up_act, hidden, down,
    ) = stored
    qkv_w, output_w = attn_w
    gate_up_w, down_w = ffn_w
    pre_g, query_g, key_g, mix_g, ffn_g, out_g = gains
    cosine, sine = tables
    d_down, by_out = norm_back(grad_out, down, out_g)
    d_out_g = jnp.sum(by_out, axis=0)
    d_down = d_down.astype(jnp.bfloat16)
    d_hidden = against(d_down, down_w)
    _, pull = jax.vjp(
        lambda gate_in, up_in: jax.nn.gelu(gate_in) * up_in, gate_act, up_act
    )
    d_gate, d_up = pull(d_hidden)
    d_gate_up = jnp.concatenate([d_gate.astype(jnp.bfloat16), d_up.astype(jnp.bfloat16)], axis=1)
    kept.update(inner=inner, d_gate_up=d_gate_up, hidden=hidden, d_down=d_down)
    d_inner = against(d_gate_up, gate_up_w)
    d_middle_ffn, by_ffn = norm_back(d_inner, middle, ffn_g)
    d_ffn_g = jnp.sum(by_ffn, axis=0)
    d_middle = grad_out + d_middle_ffn
    d_branch, by_mix = norm_back(d_middle, branch, mix_g)
    d_mix_g = jnp.sum(by_mix, axis=0)
    d_branch = d_branch.astype(jnp.bfloat16)
    d_mixed = against(d_branch, output_w).astype(jnp.bfloat16)
    kept.update(mixed=mixed, d_branch=d_branch)
    if other is not None:
        picked = {name: chosen(name, kept[name]) for name in kept}
        grad_early = (
            inner_rows(picked["inner"], picked["d_gate_up"]),
            inner_rows(picked["hidden"], picked["d_down"]),
            inner_rows(picked["mixed"], picked["d_branch"]),
        )
        early_begun = reduce_z_begin(place, grad_early, EARLY_PLAN, EARLY_COLS)
        d_mixed = ordered(d_mixed, early_begun[0])
    d_mixed = jnp.swapaxes(d_mixed.reshape(MICRO, SHARD, QH, HD), 1, 2)
    d_prob = batched("mhqd,mkd->mhqk", d_mixed, values_all)
    d_score = (prob * (d_prob - jnp.sum(prob * d_prob, axis=-1, keepdims=True))).astype(
        jnp.bfloat16
    )
    scale = HD ** (-0.5)
    d_keys = batched("mhqk,mhqd->mkd", d_score, query_rot) * scale
    if other is not None:
        d_keys = ordered(d_keys, early_begun[3], early_begun[4])
        early_parts = reduce_z_end(early_begun)
    d_values_all = batched("mhqk,mhqd->mkd", prob.astype(jnp.bfloat16), d_mixed)
    d_stacked = jnp.stack([d_keys, d_values_all])
    back = d_stacked[:, :, HOPS * SHARD :]
    for offset in range(HOPS):
        piece = d_stacked[:, :, offset * SHARD : (offset + 1) * SHARD].astype(jnp.bfloat16)
        back = back + along_seq(piece, section, offset - HOPS).astype(jnp.float32)
    back = back.reshape(2, TOKENS, HD)
    d_query_rot = batched("mhqk,mkd->mhqd", d_score, keys_all) * scale
    d_query, by_query = norm_back(
        turn(
            d_query_rot,
            cosine.reshape(MICRO, 1, SHARD, HD // 2),
            -sine.reshape(MICRO, 1, SHARD, HD // 2),
        ),
        query_raw,
        query_g,
    )
    d_query_g = jnp.sum(by_query, axis=(0, 1, 2))
    d_query = jnp.swapaxes(d_query.astype(jnp.bfloat16), 1, 2).reshape(TOKENS, QH * HD)
    d_values = back[1].astype(jnp.bfloat16)
    d_key, by_key = norm_back(turn(back[0], cosine, -sine), key_raw, key_g)
    d_key_g = jnp.sum(by_key, axis=0)
    d_qkv = jnp.concatenate([d_query, d_key.astype(jnp.bfloat16), d_values], axis=1)
    d_normed = against(d_qkv, qkv_w)
    d_inputs_pre, by_pre = norm_back(d_normed, inputs, pre_g)
    d_pre_g = jnp.sum(by_pre, axis=0)
    d_inputs = d_middle + d_inputs_pre
    wide = jnp.stack([d_pre_g, d_mix_g, d_ffn_g, d_out_g]).reshape(4, RING, D // RING)
    narrow = jnp.stack([d_query_g, d_key_g]).reshape(2, RING, HD // RING)
    rows = jnp.concatenate(
        [
            jnp.pad(jnp.swapaxes(wide, 0, 1), ((0, 0), (0, 0), (0, 512 - D // RING))),
            jnp.pad(jnp.swapaxes(narrow, 0, 1), ((0, 0), (0, 26), (0, 512 - HD // RING))),
        ],
        axis=1,
    ).astype(jnp.bfloat16)
    last = dict(normed=normed, d_qkv=d_qkv, rows=rows.reshape(RING * 32, 512))
    kept.update(last)
    if other is None:
        return d_inputs, kept
    picked = {name: chosen(name, last[name]) for name in last}
    grad_late = (inner_rows(picked["normed"], picked["d_qkv"]), picked["rows"])
    late_parts = reduce_z_end(
        reduce_z_begin(place, grad_late, LATE_PLAN, LATE_COLS, early_parts[1:])
    )
    return d_inputs, early_parts, late_parts


GAIN_SIZES = (D, HD, HD, D, D, D)
GAIN_ROWS = (0, 4, 5, 1, 2, 3)


def per_device(
    hidden_in, positions, segments, cotangent,
    query_weight, key_weight, value_weight, output_weight, gate_weight, up_weight, down_weight,
    pre_gain, query_gain, key_gain, mix_gain, ffn_gain, out_gain,
):
    leading = lax.axis_index("section") == 0
    z_index = lax.axis_index("z")
    seq_index = lax.axis_index("y") * RING + lax.axis_index("x")
    place = jnp.reshape(z_index, (1,)).astype(jnp.int32)

    wide = jnp.concatenate([pre_gain, mix_gain, ffn_gain, out_gain])
    narrow = jnp.concatenate([query_gain, key_gain])
    gain_shard = jnp.concatenate(
        [
            jnp.pad(wide, ((0, 0), (0, D - D // RING))),
            jnp.pad(narrow, ((0, 26), (0, D - HD // RING))),
        ]
    )
    attn_arrays = (query_weight[0], key_weight[0], value_weight[0], output_weight[0], gain_shard)
    ffn_arrays = (gate_weight[0], up_weight[0], down_weight[0])
    attn_pieces, passed = gather_weights(pack_shard(attn_arrays, ATTN_PLAN, ATTN_COLS))
    ffn_shard = pack_shard(ffn_arrays, FFN_PLAN, FFN_COLS, passed)
    ffn_pieces, _ = gather_weights(ffn_shard)
    qkv_w, output_w, corner = unpack_full(
        place, attn_pieces, ATTN_GRAD_PLAN, ATTN_SHAPES, (ffn_shard,)
    )
    attn_w = (qkv_w, output_w)
    corner = corner.reshape(RING, 32, D).astype(jnp.float32)
    gains = [
        corner[:, row, : size // RING].reshape(size) for row, size in zip(GAIN_ROWS, GAIN_SIZES)
    ]
    ffn_w = []

    def await_ffn(mixed):
        mixed = ordered(mixed, ffn_pieces[1][0], ffn_pieces[2][0])
        ffn_w.extend(unpack_full(place, ffn_pieces, FFN_GRAD_PLAN, FFN_SHAPES, (mixed,)))
        return mixed, ffn_w

    exponent = jnp.arange(HD // 2).astype(jnp.float32) * (2.0 / HD)
    freqs = ROPE_BASE ** (-exponent)
    angle = positions[:, 0].reshape(TOKENS).astype(jnp.float32)[:, None] * freqs[None, :]
    tables = (jnp.cos(angle), jnp.sin(angle))

    segment_rows = segments[:, 0]
    anchor = seq_index * SHARD
    padded = jnp.concatenate([jnp.full((MICRO, WINDOW), -1, jnp.int32), segment_rows], axis=1)
    query_seg = lax.dynamic_slice_in_dim(segment_rows, anchor, SHARD, 1)
    key_seg = lax.dynamic_slice_in_dim(padded, anchor, KEYS, 1)
    gap = (jnp.arange(SHARD, dtype=jnp.int32) + WINDOW)[:, None] - jnp.arange(
        KEYS, dtype=jnp.int32
    )[None, :]
    allowed = (gap >= 0) & (gap < WINDOW)
    allowed = allowed[None] & (query_seg[:, :, None] == key_seg[:, None, :])

    first_in = hidden_in[:, 0].reshape(TOKENS, D).astype(jnp.float32)
    first_out, first_kept = forward_layer(
        first_in, tables, allowed, attn_w, gains, 0, await_ffn
    )
    handed = lax.ppermute(first_out, "section", [(0, 1)]).astype(jnp.float32)
    second_out, second_kept = forward_layer(
        handed, tables, allowed, attn_w, gains, 1, lambda mixed: (mixed, ffn_w)
    )

    cot = cotangent[:, 0].reshape(TOKENS, D).astype(jnp.float32)
    d_second, left = backward_layer(cot, second_kept, tables, attn_w, ffn_w, gains, 1)
    d_first_out = lax.ppermute(d_second.astype(jnp.bfloat16), "section", [(1, 0)])
    d_first, early_parts, late_parts = backward_layer(
        d_first_out.astype(jnp.float32), first_kept, tables, attn_w, ffn_w, gains, 0,
        place, leading, left,
    )

    def finish(parts, cols):
        mine = total_of(parts).astype(jnp.bfloat16)
        count = RING * RING
        split = mine.reshape(count, ROWS // count, cols)
        moved = lax.all_to_all(split, ("y", "x"), split_axis=0, concat_axis=0, tiled=True)
        summed = jnp.sum(moved.astype(jnp.float32), axis=0).astype(jnp.bfloat16)
        return lax.all_gather(summed, ("y", "x"), axis=0, tiled=True)

    early_done = finish(early_parts, EARLY_COLS)
    late_done = finish(late_parts, LATE_COLS)
    early_outs = unpack_grads(early_done, EARLY_OUT, ((160, FF), (160, FF), (512, D), (256, D)))
    late_outs = unpack_grads(
        late_done, LATE_OUT, ((160, QH * HD), (160, HD), (160, HD), (32, 512))
    )
    gain_outs = [
        late_outs[3][row : row + 1, : size // RING] for row, size in zip(GAIN_ROWS, GAIN_SIZES)
    ]
    outputs = jnp.where(leading, first_out, second_out).reshape(1, MICRO, 1, SHARD, D)
    input_grads = jnp.where(leading, d_first, d_second).reshape(1, MICRO, 1, SHARD, D)
    return (
        outputs,
        input_grads,
        *(item[None] for item in late_outs[:3]),
        early_outs[3][None],
        *(item[None] for item in early_outs[:3]),
        *gain_outs,
    )


def solution(mesh):
    grid = Mesh(
        mesh.devices.reshape(2, RING, RING, RING), ("section", "y", "x", "z")
    )
    seq = ("y", "x")
    in_specs = (
        P(None, "z", seq, None),
        P(None, "z", seq),
        P(None, "z", None),
        P(None, "z", seq, None),
    ) + (P("section", "z", None),) * 7 + (P("section", "z"),) * 6
    out_specs = (
        (P("section", None, "z", seq, None),) * 2
        + (P("section", "z", None),) * 7
        + (P("section", "z"),) * 6
    )
    return jax.shard_map(
        per_device, mesh=grid, in_specs=in_specs, out_specs=out_specs, check_vma=False
    )
```
